32 devices in a mesh: clips: 2 (over y), ctx: 8 (over z, x), head: 2 (over core).
Axes of the slice: x: 2, y: 2, z: 4, core: 2. Of those that a mesh axis runs over, the one named last changes fastest.
Arguments:
- query_in: bfloat16 [4096, 2560], P(('clips', 'ctx', 'head')), parts along dimension 0, may hold values from -6 to 6
- key_in: bfloat16 [4096, 2560], P(('clips', 'ctx', 'head')), parts along dimension 0, may hold values from -6 to 6
- value_in: bfloat16 [4096, 2560], P(('clips', 'ctx', 'head')), parts along dimension 0, may hold values from -6 to 6
- block_keep: int32 [2, 1, 8, 3, 3], P('clips'), parts along dimension 0, may hold values 0 or 1
Outputs:
- attended: bfloat16 [4096, 2560], P(('clips', 'ctx', 'head')), parts along dimension 0
The draws below stay inside these ranges and needn't reach their ends.
There are 2 independent parts, one for each index of `clips`. The reference program is written for one: setup_inputs(seed, part) draws one part's arguments, and reference() takes and returns one part's arrays. A program takes and returns all parts, laid end to end along the dimension named above; each array names one. Nothing has to cross between parts.
All inputs are finite; a program needn't handle non-finite values.
Results may differ from the reference program's by a relative error of at most 0.0035.
Values may be sent and summed in bfloat16 or wider, within the bound.
A program may use at most 128 MiB of HBM per device.

```python
import jax
import jax.numpy as jnp
from jax import lax

HEADS = 20
HD = 128
COL_TILES = 8
ROW_TILES = 1
FRAME_TILES = 1
TILE_TOK = 256
TOKENS = 2048


def draw_query_in(key, part):
    key = jax.random.fold_in(key, 3)
    base = jnp.clip(jax.random.normal(key, (TOKENS, HEADS * HD), jnp.float32) * 1.4, -6.0, 6.0)
    return base.astype(jnp.bfloat16)


def draw_key_in(key, part):
    key = jax.random.fold_in(key, 5)
    base = jnp.clip(jax.random.normal(key, (TOKENS, HEADS * HD), jnp.float32) * 1.4, -6.0, 6.0)
    return base.astype(jnp.bfloat16)


def place_ends(values, stream_key, low, high):
    longest = values.shape.index(max(values.shape))
    spots = []
    for shift in (0, 1):
        where = [jax.random.randint(jax.random.fold_in(stream_key, axis), (), 0, length) for axis, length in enumerate(values.shape)]
        where[longest] = (where[longest] + shift) % values.shape[longest]
        spots.append(tuple(where))
    return values.at[spots[0]].set(low).at[spots[1]].set(high)


def levels(key, shape, cuts, smallest, top_value):
    def one(position, blocks):
        heights = jax.random.uniform(jax.random.fold_in(jax.random.fold_in(key, 6), position), (blocks,), jnp.float32, smallest / len(cuts), top_value / len(cuts))
        return jnp.repeat(jnp.exp(heights), shape[position] // blocks).reshape((-1,) + (1,) * (len(shape) - position - 1))

    level = one(*cuts[0])
    for cut in cuts[1:]:
        level = level * one(*cut)
    return level


def normal_values(rng, shape, deviation, reach, pieces=(), held_as=jnp.bfloat16):
    values = jax.random.normal(rng, shape, jnp.float32) * deviation
    if len(pieces) > 0:
        values = levels(rng, shape, pieces, -0.22, 0.18) * values
    return jnp.clip(values, min=-reach, max=reach).astype(held_as)


def setup_inputs(seed: int = 0, part: int = 0) -> dict:
    arg_keys = jax.random.split(jax.random.key(seed), 5)
    part_keys = jax.random.split(jax.random.fold_in(arg_keys[4], part), 5)
    return {
        "query_in": draw_query_in(jax.random.fold_in(jax.random.fold_in(arg_keys[4], part), 71), part),
        "key_in": draw_key_in(jax.random.fold_in(jax.random.fold_in(arg_keys[4], part), 71), part),
        "value_in": normal_values(part_keys[2], (TOKENS, HEADS * HD), 1.0, 6.0, ((0, 16),)),
        "block_keep": place_ends((jax.random.randint(part_keys[3], (FRAME_TILES, ROW_TILES, COL_TILES, 3, 3), 0, 4) < 3).astype(jnp.int32), jax.random.fold_in(part_keys[3], 1), 0, 1),
    }


def tile_grid(array):
    return array.reshape(FRAME_TILES, ROW_TILES, COL_TILES, TILE_TOK, HEADS, HD)


def reference(query_in, key_in, value_in, block_keep):
    tile_count = FRAME_TILES * ROW_TILES * COL_TILES
    padding = ((1, 1), (0, 0), (1, 1), (0, 0), (0, 0), (0, 0))
    key_grid = jnp.pad(tile_grid(key_in), padding)
    value_grid = jnp.pad(tile_grid(value_in), padding)
    query_tiles = query_in.reshape(tile_count, TILE_TOK, HEADS, HD)
    keep_tiles = (block_keep > 0).reshape(tile_count, 3, 3)
    frame_offset = jnp.arange(3, dtype=jnp.int32)[:, None]
    column_offset = jnp.arange(3, dtype=jnp.int32)[None, :]
    own_tile = (frame_offset == 1) & (column_offset == 1)

    def one_tile(tile_id):
        frame_tile = tile_id // (ROW_TILES * COL_TILES)
        row_tile = (tile_id // COL_TILES) % ROW_TILES
        col_tile = tile_id % COL_TILES
        anchor = jnp.zeros((), jnp.int32)
        start = (frame_tile, row_tile, col_tile, anchor, anchor, anchor)
        extent = (3, 1, 3, TILE_TOK, HEADS, HD)
        key_block = lax.dynamic_slice(key_grid, start, extent).reshape(9 * TILE_TOK, HEADS, HD).astype(jnp.float32)
        value_block = lax.dynamic_slice(value_grid, start, extent).reshape(9 * TILE_TOK, HEADS, HD).astype(jnp.float32)
        frame_ok = (frame_tile + frame_offset - 1 >= 0) & (frame_tile + frame_offset - 1 < FRAME_TILES)
        col_ok = (col_tile + column_offset - 1 >= 0) & (col_tile + column_offset - 1 < COL_TILES)
        tile_allowed = (keep_tiles[tile_id] & frame_ok & col_ok) | own_tile
        allowed = jnp.broadcast_to(tile_allowed.reshape(9, 1), (9, TILE_TOK)).reshape(9 * TILE_TOK)
        query_block = query_tiles[tile_id].astype(jnp.float32)
        scores = jnp.einsum("qhd,khd->hqk", query_block, key_block) * (HD ** -0.5)
        scores = jnp.where(allowed[None, None, :], scores, -jnp.inf)
        row_max = scores.max(-1, keepdims=True)
        weights = jnp.exp(scores - row_max)
        row_sum = weights.sum(-1)
        rounded = lax.optimization_barrier(weights.astype(jnp.bfloat16))
        mixed = jnp.einsum("hqk,khd->hqd", rounded.astype(jnp.float32), value_block)
        return (mixed / row_sum[..., None]).astype(jnp.bfloat16)

    tiles_out = lax.map(one_tile, jnp.arange(tile_count, dtype=jnp.int32))
    return tiles_out.transpose(0, 2, 1, 3).reshape(TOKENS, HEADS * HD)
```

```python
import functools

import jax
import jax.numpy as jnp
from jax import lax
from jax.experimental import pallas as pl
from jax.experimental.pallas import tpu as pltpu
from jax.sharding import PartitionSpec as P

HD = 128
TILE_S = 8
COLS = 64


NEG_BIG = -1e30


def swapped(block, axis, distance):
    count = lax.axis_size(axis)
    route = []
    for low in range(count):
        high = low | 1 << distance
        if high != low and high < count:
            route += [(low, high), (high, low)]
    return lax.ppermute(block, axis, route)


def from_behind(block, axis, distance):
    devices = range(lax.axis_size(axis))
    route = [(i - distance, i) for i in devices if i - distance in devices]
    return lax.ppermute(block, axis, route)


def order_pair(pair_side, mine, partner):
    first = jnp.where(pair_side == 0, mine, partner)
    second = jnp.where(pair_side == 0, partner, mine)
    return jnp.concatenate([first, second], axis=0)


def tile_flag(keep_pair, frame_at, col_at, frame_tiles, col_tiles, query_pos, frame_step, column):
    spot = column - query_pos + 1
    if frame_step == 1 and spot == 1:
        return jnp.array(True)
    frame_ok = (frame_at + frame_step - 1 >= 0) & (frame_at + frame_step - 1 < frame_tiles)
    col_ok = (col_at + column >= 0) & (col_at + column < col_tiles)
    return keep_pair[query_pos, frame_step, spot] & frame_ok & col_ok


def absorb(running, scores, allowed, mix_values):
    run_max, run_sum, run_out = running
    masked = jnp.where(allowed[None], scores, NEG_BIG)
    new_max = jnp.maximum(run_max, masked.max(-1))
    block_sum = jnp.where(allowed[None], jnp.exp(masked - new_max[..., None]), 0.0).sum(-1)
    weights_b = jnp.where(allowed[None], jnp.exp(masked - new_max[..., None]), 0.0).astype(
        jnp.bfloat16
    )
    factor = jnp.exp(run_max - new_max)
    new_sum = run_sum * factor + block_sum
    product = mix_values(weights_b)
    return (new_max, new_sum, run_out * factor[..., None] + product)


def inner_block(running, query_heads, key_pair, value_pair, tile_flags):
    tile_tok = key_pair.shape[0] // 2
    head_count = query_heads.shape[1]
    allowed = jnp.broadcast_to(tile_flags[:, None, :, None], (2, tile_tok, 2, tile_tok)).reshape(
        2 * tile_tok, 2 * tile_tok
    )
    key_rows = key_pair.reshape(2 * tile_tok, head_count, HD)
    value_rows = value_pair.reshape(2 * tile_tok, head_count, HD)
    scores = jnp.einsum(
        "qhd,khd->hqk", query_heads, key_rows, preferred_element_type=jnp.float32
    ) * HD ** (-0.5)

    def mix_values(weights_b):
        return jnp.einsum("hqk,khd->hqd", weights_b, value_rows, preferred_element_type=jnp.float32)

    return absorb(running, scores, allowed, mix_values)


def outer_block(running, query_heads, key_groups, value_groups, tile_flags):
    tile_tok = key_groups.shape[1]
    head_count = query_heads.shape[1]
    allowed = jnp.broadcast_to(tile_flags[:, None, None], (2, tile_tok, tile_tok)).reshape(
        2 * tile_tok, tile_tok
    )
    query_groups = query_heads.reshape(2, tile_tok, head_count, HD)
    key_rows = key_groups.reshape(2, tile_tok, head_count, HD)
    value_rows = value_groups.reshape(2, tile_tok, head_count, HD)
    scores = jnp.einsum(
        "gqhd,gkhd->hgqk", query_groups, key_rows, preferred_element_type=jnp.float32
    ) * HD ** (-0.5)
    scores = scores.reshape(head_count, 2 * tile_tok, tile_tok)

    def mix_values(weights_b):
        grouped = weights_b.reshape(head_count, 2, tile_tok, tile_tok)
        mixed = jnp.einsum(
            "hgqk,gkhd->hgqd", grouped, value_rows, preferred_element_type=jnp.float32
        )
        return mixed.reshape(head_count, 2 * tile_tok, HD)

    return absorb(running, scores, allowed, mix_values)


def local(query_in, key_in, value_in, block_keep):
    ctx_count = lax.axis_size("ctx")
    ctx_place = lax.axis_index("ctx")
    col_tiles = COLS // TILE_S
    row_tiles = max(1, ctx_count // (4 * col_tiles))
    frame_tiles = ctx_count // (row_tiles * col_tiles)
    frame_stride = row_tiles * col_tiles
    query_full, key_full, value_full = (
        lax.all_to_all(query_in, "head", split_axis=1, concat_axis=0, tiled=True),
        lax.all_to_all(key_in, "head", split_axis=1, concat_axis=0, tiled=True),
        lax.all_to_all(value_in, "head", split_axis=1, concat_axis=0, tiled=True),
    )
    tile_tok = query_full.shape[0]
    half_width = query_full.shape[1] // 2
    head_count = half_width // HD
    pair_side = ctx_place % 2

    def part_of(array, which):
        return lax.dynamic_slice_in_dim(array, which * half_width, half_width, 1)

    other_side = 1 - pair_side
    got_query, got_key, got_value = swapped(
        (
            part_of(query_full, other_side),
            part_of(key_full, other_side),
            part_of(value_full, other_side),
        ),
        "ctx",
        0,
    )
    query_pair = order_pair(pair_side, part_of(query_full, pair_side), got_query)
    key_pair = order_pair(pair_side, part_of(key_full, pair_side), got_key)
    value_pair = order_pair(pair_side, part_of(value_full, pair_side), got_value)
    query_heads = query_pair.reshape(2 * tile_tok, head_count, HD)
    first_tile = ctx_place - pair_side
    frame_at = first_tile // frame_stride
    col_at = first_tile % col_tiles
    keep_all = (block_keep > 0).reshape(-1, 3, 3)
    keep_pair = lax.dynamic_slice_in_dim(keep_all, first_tile, 2, 0)

    def inner_flags(frame_step):
        rows_list = []
        for query_pos in (0, 1):
            rows_list.append(
                jnp.stack(
                    [
                        tile_flag(
                            keep_pair,
                            frame_at,
                            col_at,
                            frame_tiles,
                            col_tiles,
                            query_pos,
                            frame_step,
                            column,
                        )
                        for column in (0, 1)
                    ]
                )
            )
        return jnp.stack(rows_list)

    def outer_flags(frame_step):
        left_flag = tile_flag(
            keep_pair, frame_at, col_at, frame_tiles, col_tiles, 0, frame_step, -1
        )
        right_flag = tile_flag(
            keep_pair, frame_at, col_at, frame_tiles, col_tiles, 1, frame_step, 2
        )
        return jnp.stack([left_flag, right_flag])

    side_tiles = []
    for distance, which_tile in ((2, 1), (-2, 0)):
        sent_tile = (
            key_pair[which_tile * tile_tok : (which_tile + 1) * tile_tok],
            value_pair[which_tile * tile_tok : (which_tile + 1) * tile_tok],
        )
        side_tiles.append(from_behind((sent_tile[0], sent_tile[1]), "ctx", distance))
    left_tile, right_tile = side_tiles
    running = (
        jnp.full((head_count, 2 * tile_tok), NEG_BIG, jnp.float32),
        jnp.zeros((head_count, 2 * tile_tok), jnp.float32),
        jnp.zeros((head_count, 2 * tile_tok, HD), jnp.float32),
    )
    running = inner_block(running, query_heads, key_pair, value_pair, inner_flags(1))
    running = outer_block(
        running,
        query_heads,
        jnp.stack([left_tile[0], right_tile[0]]),
        jnp.stack([left_tile[1], right_tile[1]]),
        outer_flags(1),
    )
    for frame_step, distance in ((0, frame_stride), (2, -frame_stride)):
        near_key, near_value = from_behind((key_pair, value_pair), "ctx", distance)
        corners = []
        for offset, which_tile in ((2, 1), (-2, 0)):
            sent_tile = (
                key_pair[which_tile * tile_tok : (which_tile + 1) * tile_tok],
                value_pair[which_tile * tile_tok : (which_tile + 1) * tile_tok],
            )
            corners.append(from_behind((sent_tile[0], sent_tile[1]), "ctx", distance + offset))
        running = inner_block(running, query_heads, near_key, near_value, inner_flags(frame_step))
        running = outer_block(
            running,
            query_heads,
            jnp.stack([corners[0][0], corners[1][0]]),
            jnp.stack([corners[0][1], corners[1][1]]),
            outer_flags(frame_step),
        )
    run_max, run_sum, run_out = running
    finished = (run_out / run_sum[..., None]).astype(jnp.bfloat16)
    finished = finished.transpose(1, 0, 2).reshape(2 * tile_tok, head_count * HD)
    first_out = finished[:tile_tok]
    second_out = finished[tile_tok:]
    mine_out = jnp.where(pair_side == 0, first_out, second_out)
    partner_out = jnp.where(pair_side == 0, second_out, first_out)
    returned = swapped(partner_out, "ctx", 0)
    whole_tile = jnp.where(
        pair_side == 0,
        jnp.concatenate([mine_out, returned], axis=1),
        jnp.concatenate([returned, mine_out], axis=1),
    )
    return lax.all_to_all(whole_tile, "head", split_axis=0, concat_axis=1, tiled=True)


HEADS_A_CHUNK = 2
LOG2_E = 1.4426950408889634
MESH = pl.DeviceIdType.MESH
OWN, CORE, BESIDE, BESIDE_CORE, FAR, FAR_CORE = range(6)


def attend(query, keys, values, beside_ok, far_ok, tile_tok):
    scale = HD ** (-0.5) * LOG2_E
    scores = lax.dot_general(
        query, keys, (((1,), (1,)), ((), ())), preferred_element_type=jnp.float32
    )
    own, beside, far = (scores[:, i * tile_tok : (i + 1) * tile_tok] for i in range(3))
    row_max = jnp.maximum(
        own.max(-1, keepdims=True),
        jnp.maximum(
            jnp.where(beside_ok, beside.max(-1, keepdims=True), NEG_BIG),
            jnp.where(far_ok, far.max(-1, keepdims=True), NEG_BIG),
        ),
    )
    weights = jnp.concatenate(
        [
            jnp.exp2((own - row_max) * scale),
            jnp.exp2((beside - jnp.where(beside_ok, row_max, -NEG_BIG)) * scale),
            jnp.exp2((far - jnp.where(far_ok, row_max, -NEG_BIG)) * scale),
        ],
        axis=1,
    )
    row_sum = weights.sum(-1, keepdims=True)
    mixed = jnp.dot(weights.astype(jnp.bfloat16), values, preferred_element_type=jnp.float32)
    return (mixed / row_sum).astype(jnp.bfloat16)


def row_kernel(
    tiles, heads_a_chunk,
    query_in, key_in, value_in, keep, out,
    query, pairs, result, load_sem, store_sem, send_sem, recv_sem,
):
    rows = query_in.shape[0]
    chunks = query_in.shape[1] // (heads_a_chunk * HD)
    width = heads_a_chunk * HD
    clip, tile, core = lax.axis_index("clips"), lax.axis_index("ctx"), lax.axis_index("head")
    side = lax.rem(tile, 2)
    step = 2 - 4 * side
    to_far, from_far = tile + step, tile - step
    sends_far = jnp.logical_and(to_far >= 0, to_far < tiles)
    gets_far = jnp.logical_and(from_far >= 0, from_far < tiles)
    other_core = (clip, tile, 1 - core)
    paired = (clip, tile + 1 - 2 * side, core)
    beyond = (clip, jnp.where(sends_far, to_far, tile), core)
    behind = (clip, jnp.where(gets_far, from_far, tile), core)

    def place(slot):
        return pl.ds(slot * rows, rows)

    def columns(chunk):
        return pl.ds(pl.multiple_of(chunk * width, width), width)

    def own_copy(which, kind, slot, device, chunk):
        source = (key_in, value_in)[which]
        return pltpu.make_async_remote_copy(
            src_ref=source.at[:, columns(chunk)],
            dst_ref=pairs.at[which, place(slot), columns(chunk)],
            send_sem=send_sem.at[kind + which, chunk],
            recv_sem=recv_sem.at[kind + which, chunk],
            device_id=device,
            device_id_type=MESH,
        )

    def relay(kind, source, slot, device, chunk):
        return pltpu.make_async_remote_copy(
            src_ref=pairs.at[:, place(source), columns(chunk)],
            dst_ref=pairs.at[:, place(slot), columns(chunk)],
            send_sem=send_sem.at[kind, chunk],
            recv_sem=recv_sem.at[kind, chunk],
            device_id=device,
            device_id_type=MESH,
        )

    def to_core(which, chunk):
        return own_copy(which, 0, CORE, other_core, chunk)

    def to_paired(which, chunk):
        return own_copy(which, 2, BESIDE, paired, chunk)

    def paired_to_core(chunk):
        return relay(4, BESIDE, BESIDE_CORE, other_core, chunk)

    def paired_to_far(chunk):
        return relay(5, BESIDE, FAR, beyond, chunk)

    def far_to_core(chunk):
        return relay(6, FAR, FAR_CORE, other_core, chunk)

    def store(chunk):
        return pltpu.make_async_copy(
            result.at[:, columns(chunk)], out.at[:, columns(chunk)], store_sem.at[chunk]
        )

    loads = (
        pltpu.make_async_copy(query_in, query, load_sem.at[0]),
        pltpu.make_async_copy(key_in, pairs.at[0, place(OWN)], load_sem.at[1]),
        pltpu.make_async_copy(value_in, pairs.at[1, place(OWN)], load_sem.at[2]),
    )

    barrier = pltpu.get_barrier_semaphore()
    pl.semaphore_signal(barrier, inc=1, device_id=other_core, device_id_type=MESH)
    pl.semaphore_signal(barrier, inc=1, device_id=paired, device_id_type=MESH)

    @pl.when(sends_far)
    def _():
        pl.semaphore_signal(barrier, inc=1, device_id=beyond, device_id_type=MESH)

    @pl.when(gets_far)
    def _():
        pl.semaphore_signal(barrier, inc=1, device_id=behind, device_id_type=MESH)

    for load in loads:
        load.start()

    @pl.when(jnp.logical_not(gets_far))
    def _():
        pairs[:, pl.ds(FAR * rows, 2 * rows), :] = jnp.zeros(
            (2, 2 * rows, pairs.shape[2]), pairs.dtype
        )

    pl.semaphore_wait(
        barrier, 2 + sends_far.astype(jnp.int32) + gets_far.astype(jnp.int32)
    )

    @pl.loop(0, chunks)
    def _(chunk):
        for which in range(2):
            to_paired(which, chunk).start()
        for which in range(2):
            to_core(which, chunk).start()

    for load in loads:
        load.wait()

    beside_ok = jnp.where(side == 0, keep[0, 0, tile, 1, 2], keep[0, 0, tile, 1, 0]) > 0
    far_ok = jnp.logical_and(
        jnp.where(side == 0, keep[0, 0, tile, 1, 0], keep[0, 0, tile, 1, 2]) > 0, gets_far
    )

    @pl.loop(0, chunks + 2)
    def _(turn):
        @pl.when(turn < chunks)
        def _():
            for which in range(2):
                to_paired(which, turn).wait_recv()
            paired_to_core(turn).start()

            @pl.when(sends_far)
            def _():
                paired_to_far(turn).start()

        @pl.when(jnp.logical_and(jnp.logical_and(turn >= 1, turn <= chunks), gets_far))
        def _():
            paired_to_far(turn - 1).wait_recv()
            far_to_core(turn - 1).start()

        @pl.when(turn >= 2)
        def _():
            chunk = turn - 2
            for which in range(2):
                to_core(which, chunk).wait_recv()
            paired_to_core(chunk).wait_recv()

            @pl.when(gets_far)
            def _():
                far_to_core(chunk).wait_recv()

            for head in range(heads_a_chunk):
                at = pl.ds(pl.multiple_of(chunk * width + head * HD, HD), HD)
                result[:, at] = attend(
                    query[:, at], pairs[0, :, at], pairs[1, :, at], beside_ok, far_ok, 2 * rows
                )
            store(chunk).start()

    @pl.loop(0, chunks)
    def _(chunk):
        for which in range(2):
            to_core(which, chunk).wait_send()
            to_paired(which, chunk).wait_send()
        paired_to_core(chunk).wait_send()

        @pl.when(sends_far)
        def _():
            paired_to_far(chunk).wait_send()

        @pl.when(gets_far)
        def _():
            far_to_core(chunk).wait_send()

        store(chunk).wait()


def one_row(query_in, key_in, value_in, block_keep):
    rows, width = query_in.shape
    heads = width // HD
    heads_a_chunk = HEADS_A_CHUNK
    chunks = heads // heads_a_chunk
    return pl.pallas_call(
        functools.partial(row_kernel, lax.axis_size("ctx"), heads_a_chunk),
        out_shape=jax.ShapeDtypeStruct((rows, width), jnp.bfloat16),
        in_specs=[pl.BlockSpec(memory_space=pl.ANY)] * 3
        + [pl.BlockSpec(memory_space=pltpu.SMEM)],
        out_specs=pl.BlockSpec(memory_space=pl.ANY),
        scratch_shapes=[
            pltpu.VMEM((rows, width), jnp.bfloat16),
            pltpu.VMEM((2, 6 * rows, width), jnp.bfloat16),
            pltpu.VMEM((rows, width), jnp.bfloat16),
            pltpu.SemaphoreType.DMA((3,)),
            pltpu.SemaphoreType.DMA((chunks,)),
            pltpu.SemaphoreType.DMA((7, chunks)),
            pltpu.SemaphoreType.DMA((7, chunks)),
        ],
        compiler_params=pltpu.CompilerParams(
            collective_id=0, has_side_effects=True, vmem_limit_bytes=48 * 2**20
        ),
        cost_estimate=pl.CostEstimate(
            flops=24 * rows * rows * width,
            bytes_accessed=10 * rows * width,
            transcendentals=6 * rows * rows * heads,
        ),
    )(query_in, key_in, value_in, block_keep)


def solution(mesh):
    in_one_row = mesh.shape["ctx"] == COLS // TILE_S
    return jax.shard_map(
        one_row if in_one_row else local,
        mesh=mesh,
        in_specs=(
            P(("clips", "ctx", "head"), None),
            P(("clips", "ctx", "head"), None),
            P(("clips", "ctx", "head"), None),
            P("clips", None, None, None, None),
        ),
        out_specs=P(("clips", "ctx", "head"), None),
        check_vma=False,
    )
```

```python
import functools

import jax
import jax.numpy as jnp
from jax import lax
from jax.experimental import pallas as pl
from jax.experimental.pallas import tpu as pltpu
from jax.sharding import PartitionSpec as P

HD = 128
TILE_S = 8
COLS = 64


NEG_BIG = -1e30


def swapped(block, axis, distance):
    count = lax.axis_size(axis)
    route = []
    for low in range(count):
        high = low | 1 << distance
        if high != low and high < count:
            route += [(low, high), (high, low)]
    return lax.ppermute(block, axis, route)


def from_behind(block, axis, distance):
    devices = range(lax.axis_size(axis))
    route = [(i - distance, i) for i in devices if i - distance in devices]
    return lax.ppermute(block, axis, route)


def order_pair(pair_side, mine, partner):
    first = jnp.where(pair_side == 0, mine, partner)
    second = jnp.where(pair_side == 0, partner, mine)
    return jnp.concatenate([first, second], axis=0)


def tile_flag(keep_pair, frame_at, col_at, frame_tiles, col_tiles, query_pos, frame_step, column):
    spot = column - query_pos + 1
    if frame_step == 1 and spot == 1:
        return jnp.array(True)
    frame_ok = (frame_at + frame_step - 1 >= 0) & (frame_at + frame_step - 1 < frame_tiles)
    col_ok = (col_at + column >= 0) & (col_at + column < col_tiles)
    return keep_pair[query_pos, frame_step, spot] & frame_ok & col_ok


def absorb(running, scores, allowed, mix_values):
    run_max, run_sum, run_out = running
    masked = jnp.where(allowed[None], scores, NEG_BIG)
    new_max = jnp.maximum(run_max, masked.max(-1))
    block_sum = jnp.where(allowed[None], jnp.exp(masked - new_max[..., None]), 0.0).sum(-1)
    weights_b = jnp.where(allowed[None], jnp.exp(masked - new_max[..., None]), 0.0).astype(
        jnp.bfloat16
    )
    factor = jnp.exp(run_max - new_max)
    new_sum = run_sum * factor + block_sum
    product = mix_values(weights_b)
    return (new_max, new_sum, run_out * factor[..., None] + product)


def inner_block(running, query_heads, key_pair, value_pair, tile_flags):
    tile_tok = key_pair.shape[0] // 2
    head_count = query_heads.shape[1]
    allowed = jnp.broadcast_to(tile_flags[:, None, :, None], (2, tile_tok, 2, tile_tok)).reshape(
        2 * tile_tok, 2 * tile_tok
    )
    key_rows = key_pair.reshape(2 * tile_tok, head_count, HD)
    value_rows = value_pair.reshape(2 * tile_tok, head_count, HD)
    scores = jnp.einsum(
        "qhd,khd->hqk", query_heads, key_rows, preferred_element_type=jnp.float32
    ) * HD ** (-0.5)

    def mix_values(weights_b):
        return jnp.einsum("hqk,khd->hqd", weights_b, value_rows, preferred_element_type=jnp.float32)

    return absorb(running, scores, allowed, mix_values)


def outer_block(running, query_heads, key_groups, value_groups, tile_flags):
    tile_tok = key_groups.shape[1]
    head_count = query_heads.shape[1]
    allowed = jnp.broadcast_to(tile_flags[:, None, None], (2, tile_tok, tile_tok)).reshape(
        2 * tile_tok, tile_tok
    )
    query_groups = query_heads.reshape(2, tile_tok, head_count, HD)
    key_rows = key_groups.reshape(2, tile_tok, head_count, HD)
    value_rows = value_groups.reshape(2, tile_tok, head_count, HD)
    scores = jnp.einsum(
        "gqhd,gkhd->hgqk", query_groups, key_rows, preferred_element_type=jnp.float32
    ) * HD ** (-0.5)
    scores = scores.reshape(head_count, 2 * tile_tok, tile_tok)

    def mix_values(weights_b):
        grouped = weights_b.reshape(head_count, 2, tile_tok, tile_tok)
        mixed = jnp.einsum(
            "hgqk,gkhd->hgqd", grouped, value_rows, preferred_element_type=jnp.float32
        )
        return mixed.reshape(head_count, 2 * tile_tok, HD)

    return absorb(running, scores, allowed, mix_values)


def local(query_in, key_in, value_in, block_keep):
    ctx_count = lax.axis_size("ctx")
    ctx_place = lax.axis_index("ctx")
    col_tiles = COLS // TILE_S
    row_tiles = max(1, ctx_count // (4 * col_tiles))
    frame_tiles = ctx_count // (row_tiles * col_tiles)
    frame_stride = row_tiles * col_tiles
    query_full, key_full, value_full = (
        lax.all_to_all(query_in, "head", split_axis=1, concat_axis=0, tiled=True),
        lax.all_to_all(key_in, "head", split_axis=1, concat_axis=0, tiled=True),
        lax.all_to_all(value_in, "head", split_axis=1, concat_axis=0, tiled=True),
    )
    tile_tok = query_full.shape[0]
    half_width = query_full.shape[1] // 2
    head_count = half_width // HD
    pair_side = ctx_place % 2

    def part_of(array, which):
        return lax.dynamic_slice_in_dim(array, which * half_width, half_width, 1)

    other_side = 1 - pair_side
    got_query, got_key, got_value = swapped(
        (
            part_of(query_full, other_side),
            part_of(key_full, other_side),
            part_of(value_full, other_side),
        ),
        "ctx",
        0,
    )
    query_pair = order_pair(pair_side, part_of(query_full, pair_side), got_query)
    key_pair = order_pair(pair_side, part_of(key_full, pair_side), got_key)
    value_pair = order_pair(pair_side, part_of(value_full, pair_side), got_value)
    query_heads = query_pair.reshape(2 * tile_tok, head_count, HD)
    first_tile = ctx_place - pair_side
    frame_at = first_tile // frame_stride
    col_at = first_tile % col_tiles
    keep_all = (block_keep > 0).reshape(-1, 3, 3)
    keep_pair = lax.dynamic_slice_in_dim(keep_all, first_tile, 2, 0)

    def inner_flags(frame_step):
        rows_list = []
        for query_pos in (0, 1):
            rows_list.append(
                jnp.stack(
                    [
                        tile_flag(
                            keep_pair,
                            frame_at,
                            col_at,
                            frame_tiles,
                            col_tiles,
                            query_pos,
                            frame_step,
                            column,
                        )
                        for column in (0, 1)
                    ]
                )
            )
        return jnp.stack(rows_list)

    def outer_flags(frame_step):
        left_flag = tile_flag(
            keep_pair, frame_at, col_at, frame_tiles, col_tiles, 0, frame_step, -1
        )
        right_flag = tile_flag(
            keep_pair, frame_at, col_at, frame_tiles, col_tiles, 1, frame_step, 2
        )
        return jnp.stack([left_flag, right_flag])

    side_tiles = []
    for distance, which_tile in ((2, 1), (-2, 0)):
        sent_tile = (
            key_pair[which_tile * tile_tok : (which_tile + 1) * tile_tok],
            value_pair[which_tile * tile_tok : (which_tile + 1) * tile_tok],
        )
        side_tiles.append(from_behind((sent_tile[0], sent_tile[1]), "ctx", distance))
    left_tile, right_tile = side_tiles
    running = (
        jnp.full((head_count, 2 * tile_tok), NEG_BIG, jnp.float32),
        jnp.zeros((head_count, 2 * tile_tok), jnp.float32),
        jnp.zeros((head_count, 2 * tile_tok, HD), jnp.float32),
    )
    running = inner_block(running, query_heads, key_pair, value_pair, inner_flags(1))
    running = outer_block(
        running,
        query_heads,
        jnp.stack([left_tile[0], right_tile[0]]),
        jnp.stack([left_tile[1], right_tile[1]]),
        outer_flags(1),
    )
    for frame_step, distance in ((0, frame_stride), (2, -frame_stride)):
        near_key, near_value = from_behind((key_pair, value_pair), "ctx", distance)
        corners = []
        for offset, which_tile in ((2, 1), (-2, 0)):
            sent_tile = (
                key_pair[which_tile * tile_tok : (which_tile + 1) * tile_tok],
                value_pair[which_tile * tile_tok : (which_tile + 1) * tile_tok],
            )
            corners.append(from_behind((sent_tile[0], sent_tile[1]), "ctx", distance + offset))
        running = inner_block(running, query_heads, near_key, near_value, inner_flags(frame_step))
        running = outer_block(
            running,
            query_heads,
            jnp.stack([corners[0][0], corners[1][0]]),
            jnp.stack([corners[0][1], corners[1][1]]),
            outer_flags(frame_step),
        )
    run_max, run_sum, run_out = running
    finished = (run_out / run_sum[..., None]).astype(jnp.bfloat16)
    finished = finished.transpose(1, 0, 2).reshape(2 * tile_tok, head_count * HD)
    first_out = finished[:tile_tok]
    second_out = finished[tile_tok:]
    mine_out = jnp.where(pair_side == 0, first_out, second_out)
    partner_out = jnp.where(pair_side == 0, second_out, first_out)
    returned = swapped(partner_out, "ctx", 0)
    whole_tile = jnp.where(
        pair_side == 0,
        jnp.concatenate([mine_out, returned], axis=1),
        jnp.concatenate([returned, mine_out], axis=1),
    )
    return lax.all_to_all(whole_tile, "head", split_axis=0, concat_axis=1, tiled=True)


HEADS_A_CHUNK = 2
VMEM_LIMIT = 60 * 2**20
LOG2_E = 1.4426950408889634
MESH = pl.DeviceIdType.MESH
OWN, CORE, BESIDE, FAR, BESIDE_CORE, FAR_CORE = range(6)


def attend(query, keys, values, beside_ok, far_ok, rows):
    scale = HD ** (-0.5) * LOG2_E
    scores = lax.dot_general(
        query, keys, (((1,), (1,)), ((), ())), preferred_element_type=jnp.float32
    )
    halves = [scores[:, slot * rows : (slot + 1) * rows] for slot in range(6)]
    own = jnp.maximum(halves[OWN], halves[CORE])
    beside = jnp.maximum(halves[BESIDE], halves[BESIDE_CORE])
    far = jnp.maximum(halves[FAR], halves[FAR_CORE])
    row_max = jnp.maximum(
        own, jnp.maximum(jnp.where(beside_ok, beside, NEG_BIG), jnp.where(far_ok, far, NEG_BIG))
    ).max(-1, keepdims=True)
    beside_max = jnp.where(beside_ok, row_max, -NEG_BIG)
    far_max = jnp.where(far_ok, row_max, -NEG_BIG)
    tops = (row_max, row_max, beside_max, far_max, beside_max, far_max)
    weights = [jnp.exp2((half - top) * scale) for half, top in zip(halves, tops)]
    row_sum = sum(weights[1:], weights[0]).sum(-1, keepdims=True)
    weights_b = jnp.concatenate([w.astype(jnp.bfloat16) for w in weights], axis=1)
    mixed = jnp.dot(weights_b, values, preferred_element_type=jnp.float32)
    return (mixed / row_sum).astype(jnp.bfloat16)


def row_kernel(
    tiles, heads_a_chunk,
    query_in, key_in, value_in, keep, out,
    query, pairs, result, load_sem, store_sem, send_sem, core_sem, paired_sem, far_sem, relay_sem,
):
    rows = query_in.shape[0]
    chunks = query_in.shape[1] // (heads_a_chunk * HD)
    width = heads_a_chunk * HD
    clip, tile, core = lax.axis_index("clips"), lax.axis_index("ctx"), lax.axis_index("head")
    side = lax.rem(tile, 2)
    step = 2 - 4 * side
    to_far, from_far = tile + step, tile - step
    sends_far = jnp.logical_and(to_far >= 0, to_far < tiles)
    gets_far = jnp.logical_and(from_far >= 0, from_far < tiles)
    other_core = (clip, tile, 1 - core)
    paired = (clip, tile + 1 - 2 * side, core)
    beyond = (clip, jnp.where(sends_far, to_far, tile + 1 - 2 * side), core)
    behind = (clip, jnp.where(gets_far, from_far, tile + 1 - 2 * side), core)

    def place(slot, count=1):
        return pl.ds(slot * rows, count * rows)

    def columns(chunk):
        return pl.ds(pl.multiple_of(chunk * width, width), width)

    everything = slice(None)

    def own_copy(which, slot, device, at, sender, receiver):
        return pltpu.make_async_remote_copy(
            src_ref=(key_in, value_in)[which].at[:, at],
            dst_ref=pairs.at[which, place(slot), at],
            send_sem=send_sem.at[sender],
            recv_sem=receiver,
            device_id=device,
            device_id_type=MESH,
        )

    def relay(source, slot, count, device, at, sender, receiver):
        return pltpu.make_async_remote_copy(
            src_ref=pairs.at[:, place(source, count), at],
            dst_ref=pairs.at[:, place(slot, count), at],
            send_sem=send_sem.at[sender],
            recv_sem=receiver,
            device_id=device,
            device_id_type=MESH,
        )

    def to_far_tile(chunk):
        return relay(BESIDE, FAR, 1, beyond, columns(chunk), 2, far_sem.at[chunk])

    def to_other_core(chunk):
        return relay(BESIDE, BESIDE_CORE, 2, other_core, columns(chunk), 3, relay_sem.at[chunk])

    def both_arrived(slot, at, receiver):
        relay(slot, slot, 1, paired, at, 0, receiver).wait_recv()

    def store(at):
        return pltpu.make_async_copy(result.at[:, at], out.at[:, at], store_sem)

    loads = (
        pltpu.make_async_copy(query_in, query, load_sem.at[0]),
        pltpu.make_async_copy(key_in, pairs.at[0, place(OWN)], load_sem.at[1]),
        pltpu.make_async_copy(value_in, pairs.at[1, place(OWN)], load_sem.at[2]),
    )

    barrier = pltpu.get_barrier_semaphore()
    pl.semaphore_signal(barrier, inc=1, device_id=paired, device_id_type=MESH)

    @pl.when(sends_far)
    def _():
        pl.semaphore_signal(barrier, inc=1, device_id=beyond, device_id_type=MESH)

    @pl.when(gets_far)
    def _():
        pl.semaphore_signal(barrier, inc=1, device_id=behind, device_id_type=MESH)

    pl.semaphore_signal(barrier, inc=1, device_id=other_core, device_id_type=MESH)

    for load in loads:
        load.start()

    @pl.when(jnp.logical_not(gets_far))
    def _():
        pairs[:, place(FAR), :] = jnp.zeros((2, rows, pairs.shape[2]), pairs.dtype)

    pl.semaphore_wait(
        barrier, 2 + sends_far.astype(jnp.int32) + gets_far.astype(jnp.int32)
    )

    @pl.loop(0, chunks)
    def _(chunk):
        for which in range(2):
            own_copy(which, BESIDE, paired, columns(chunk), 0, paired_sem.at[chunk]).start()

    for which in range(2):
        own_copy(which, CORE, other_core, everything, 1, core_sem).start()

    beside_ok = jnp.where(side == 0, keep[0, 1, 2, 0, tile], keep[0, 1, 0, 0, tile]) > 0
    far_ok = jnp.logical_and(
        jnp.where(side == 0, keep[0, 1, 0, 0, tile], keep[0, 1, 2, 0, tile]) > 0, gets_far
    )

    for load in loads:
        load.wait()
    both_arrived(CORE, everything, core_sem)

    @pl.loop(0, chunks + 2)
    def _(turn):
        @pl.when(turn < chunks)
        def _():
            both_arrived(BESIDE, columns(turn), paired_sem.at[turn])

            @pl.when(sends_far)
            def _():
                to_far_tile(turn).start()

        @pl.when(jnp.logical_and(turn >= 1, turn <= chunks))
        def _():
            @pl.when(gets_far)
            def _():
                to_far_tile(turn - 1).wait_recv()

            to_other_core(turn - 1).start()

        @pl.when(turn >= 2)
        def _():
            chunk = turn - 2
            to_other_core(chunk).wait_recv()
            for head in range(heads_a_chunk):
                at = pl.ds(pl.multiple_of(chunk * width + head * HD, HD), HD)
                result[:, at] = attend(
                    query[:, at], pairs[0, :, at], pairs[1, :, at], beside_ok, far_ok, rows
                )
            store(columns(chunk)).start()

    relay(BESIDE, BESIDE, 1, paired, everything, 0, core_sem).wait_send()
    relay(BESIDE, BESIDE, 1, paired, everything, 1, core_sem).wait_send()
    relay(BESIDE, BESIDE, 2, paired, everything, 3, core_sem).wait_send()

    @pl.when(sends_far)
    def _():
        relay(BESIDE, BESIDE, 1, paired, everything, 2, core_sem).wait_send()

    store(everything).wait()


def one_row(query_in, key_in, value_in, block_keep):
    rows, width = query_in.shape
    heads = width // HD
    heads_a_chunk = HEADS_A_CHUNK
    chunks = heads // heads_a_chunk
    return pl.pallas_call(
        functools.partial(row_kernel, lax.axis_size("ctx"), heads_a_chunk),
        out_shape=pltpu.VMEM((rows, width), jnp.bfloat16),
        in_specs=[pl.BlockSpec(memory_space=pl.ANY)] * 3
        + [pl.BlockSpec(memory_space=pltpu.SMEM)],
        out_specs=pl.BlockSpec(memory_space=pl.ANY),
        scratch_shapes=[
            pltpu.VMEM((rows, width), jnp.bfloat16),
            pltpu.VMEM((2, 6 * rows, width), jnp.bfloat16),
            pltpu.VMEM((rows, width), jnp.bfloat16),
            pltpu.SemaphoreType.DMA((3,)),
            pltpu.SemaphoreType.DMA,
            pltpu.SemaphoreType.DMA((4,)),
            pltpu.SemaphoreType.DMA,
            pltpu.SemaphoreType.DMA((chunks,)),
            pltpu.SemaphoreType.DMA((chunks,)),
            pltpu.SemaphoreType.DMA((chunks,)),
        ],
        compiler_params=pltpu.CompilerParams(
            collective_id=0, has_side_effects=True, vmem_limit_bytes=VMEM_LIMIT
        ),
        cost_estimate=pl.CostEstimate(
            flops=24 * rows * rows * width,
            bytes_accessed=10 * rows * width,
            transcendentals=6 * rows * rows * heads,
        ),
    )(query_in, key_in, value_in, block_keep.transpose(0, 3, 4, 1, 2))


def solution(mesh):
    in_one_row = mesh.shape["ctx"] == COLS // TILE_S
    return jax.shard_map(
        one_row if in_one_row else local,
        mesh=mesh,
        in_specs=(
            P(("clips", "ctx", "head"), None),
            P(("clips", "ctx", "head"), None),
            P(("clips", "ctx", "head"), None),
            P("clips", None, None, None, None),
        ),
        out_specs=P(("clips", "ctx", "head"), None),
        check_vma=False,
    )
```

```python
import functools

import jax
import jax.numpy as jnp
from jax import lax
from jax.experimental import pallas as pl
from jax.experimental.pallas import tpu as pltpu
from jax.sharding import PartitionSpec as P

HD = 128
TILE_S = 8
COLS = 64


NEG_BIG = -1e30


def swapped(block, axis, distance):
    count = lax.axis_size(axis)
    route = []
    for low in range(count):
        high = low | 1 << distance
        if high != low and high < count:
            route += [(low, high), (high, low)]
    return lax.ppermute(block, axis, route)


def from_behind(block, axis, distance):
    devices = range(lax.axis_size(axis))
    route = [(i - distance, i) for i in devices if i - distance in devices]
    return lax.ppermute(block, axis, route)


def order_pair(pair_side, mine, partner):
    first = jnp.where(pair_side == 0, mine, partner)
    second = jnp.where(pair_side == 0, partner, mine)
    return jnp.concatenate([first, second], axis=0)


def tile_flag(keep_pair, frame_at, col_at, frame_tiles, col_tiles, query_pos, frame_step, column):
    spot = column - query_pos + 1
    if frame_step == 1 and spot == 1:
        return jnp.array(True)
    frame_ok = (frame_at + frame_step - 1 >= 0) & (frame_at + frame_step - 1 < frame_tiles)
    col_ok = (col_at + column >= 0) & (col_at + column < col_tiles)
    return keep_pair[query_pos, frame_step, spot] & frame_ok & col_ok


def absorb(running, scores, allowed, mix_values):
    run_max, run_sum, run_out = running
    masked = jnp.where(allowed[None], scores, NEG_BIG)
    new_max = jnp.maximum(run_max, masked.max(-1))
    block_sum = jnp.where(allowed[None], jnp.exp(masked - new_max[..., None]), 0.0).sum(-1)
    weights_b = jnp.where(allowed[None], jnp.exp(masked - new_max[..., None]), 0.0).astype(
        jnp.bfloat16
    )
    factor = jnp.exp(run_max - new_max)
    new_sum = run_sum * factor + block_sum
    product = mix_values(weights_b)
    return (new_max, new_sum, run_out * factor[..., None] + product)


def inner_block(running, query_heads, key_pair, value_pair, tile_flags):
    tile_tok = key_pair.shape[0] // 2
    head_count = query_heads.shape[1]
    allowed = jnp.broadcast_to(tile_flags[:, None, :, None], (2, tile_tok, 2, tile_tok)).reshape(
        2 * tile_tok, 2 * tile_tok
    )
    key_rows = key_pair.reshape(2 * tile_tok, head_count, HD)
    value_rows = value_pair.reshape(2 * tile_tok, head_count, HD)
    scores = jnp.einsum(
        "qhd,khd->hqk", query_heads, key_rows, preferred_element_type=jnp.float32
    ) * HD ** (-0.5)

    def mix_values(weights_b):
        return jnp.einsum("hqk,khd->hqd", weights_b, value_rows, preferred_element_type=jnp.float32)

    return absorb(running, scores, allowed, mix_values)


def outer_block(running, query_heads, key_groups, value_groups, tile_flags):
    tile_tok = key_groups.shape[1]
    head_count = query_heads.shape[1]
    allowed = jnp.broadcast_to(tile_flags[:, None, None], (2, tile_tok, tile_tok)).reshape(
        2 * tile_tok, tile_tok
    )
    query_groups = query_heads.reshape(2, tile_tok, head_count, HD)
    key_rows = key_groups.reshape(2, tile_tok, head_count, HD)
    value_rows = value_groups.reshape(2, tile_tok, head_count, HD)
    scores = jnp.einsum(
        "gqhd,gkhd->hgqk", query_groups, key_rows, preferred_element_type=jnp.float32
    ) * HD ** (-0.5)
    scores = scores.reshape(head_count, 2 * tile_tok, tile_tok)

    def mix_values(weights_b):
        grouped = weights_b.reshape(head_count, 2, tile_tok, tile_tok)
        mixed = jnp.einsum(
            "hgqk,gkhd->hgqd", grouped, value_rows, preferred_element_type=jnp.float32
        )
        return mixed.reshape(head_count, 2 * tile_tok, HD)

    return absorb(running, scores, allowed, mix_values)


def local(query_in, key_in, value_in, block_keep):
    ctx_count = lax.axis_size("ctx")
    ctx_place = lax.axis_index("ctx")
    col_tiles = COLS // TILE_S
    row_tiles = max(1, ctx_count // (4 * col_tiles))
    frame_tiles = ctx_count // (row_tiles * col_tiles)
    frame_stride = row_tiles * col_tiles
    query_full, key_full, value_full = (
        lax.all_to_all(query_in, "head", split_axis=1, concat_axis=0, tiled=True),
        lax.all_to_all(key_in, "head", split_axis=1, concat_axis=0, tiled=True),
        lax.all_to_all(value_in, "head", split_axis=1, concat_axis=0, tiled=True),
    )
    tile_tok = query_full.shape[0]
    half_width = query_full.shape[1] // 2
    head_count = half_width // HD
    pair_side = ctx_place % 2

    def part_of(array, which):
        return lax.dynamic_slice_in_dim(array, which * half_width, half_width, 1)

    other_side = 1 - pair_side
    got_query, got_key, got_value = swapped(
        (
            part_of(query_full, other_side),
            part_of(key_full, other_side),
            part_of(value_full, other_side),
        ),
        "ctx",
        0,
    )
    query_pair = order_pair(pair_side, part_of(query_full, pair_side), got_query)
    key_pair = order_pair(pair_side, part_of(key_full, pair_side), got_key)
    value_pair = order_pair(pair_side, part_of(value_full, pair_side), got_value)
    query_heads = query_pair.reshape(2 * tile_tok, head_count, HD)
    first_tile = ctx_place - pair_side
    frame_at = first_tile // frame_stride
    col_at = first_tile % col_tiles
    keep_all = (block_keep > 0).reshape(-1, 3, 3)
    keep_pair = lax.dynamic_slice_in_dim(keep_all, first_tile, 2, 0)

    def inner_flags(frame_step):
        rows_list = []
        for query_pos in (0, 1):
            rows_list.append(
                jnp.stack(
                    [
                        tile_flag(
                            keep_pair,
                            frame_at,
                            col_at,
                            frame_tiles,
                            col_tiles,
                            query_pos,
                            frame_step,
                            column,
                        )
                        for column in (0, 1)
                    ]
                )
            )
        return jnp.stack(rows_list)

    def outer_flags(frame_step):
        left_flag = tile_flag(
            keep_pair, frame_at, col_at, frame_tiles, col_tiles, 0, frame_step, -1
        )
        right_flag = tile_flag(
            keep_pair, frame_at, col_at, frame_tiles, col_tiles, 1, frame_step, 2
        )
        return jnp.stack([left_flag, right_flag])

    side_tiles = []
    for distance, which_tile in ((2, 1), (-2, 0)):
        sent_tile = (
            key_pair[which_tile * tile_tok : (which_tile + 1) * tile_tok],
            value_pair[which_tile * tile_tok : (which_tile + 1) * tile_tok],
        )
        side_tiles.append(from_behind((sent_tile[0], sent_tile[1]), "ctx", distance))
    left_tile, right_tile = side_tiles
    running = (
        jnp.full((head_count, 2 * tile_tok), NEG_BIG, jnp.float32),
        jnp.zeros((head_count, 2 * tile_tok), jnp.float32),
        jnp.zeros((head_count, 2 * tile_tok, HD), jnp.float32),
    )
    running = inner_block(running, query_heads, key_pair, value_pair, inner_flags(1))
    running = outer_block(
        running,
        query_heads,
        jnp.stack([left_tile[0], right_tile[0]]),
        jnp.stack([left_tile[1], right_tile[1]]),
        outer_flags(1),
    )
    for frame_step, distance in ((0, frame_stride), (2, -frame_stride)):
        near_key, near_value = from_behind((key_pair, value_pair), "ctx", distance)
        corners = []
        for offset, which_tile in ((2, 1), (-2, 0)):
            sent_tile = (
                key_pair[which_tile * tile_tok : (which_tile + 1) * tile_tok],
                value_pair[which_tile * tile_tok : (which_tile + 1) * tile_tok],
            )
            corners.append(from_behind((sent_tile[0], sent_tile[1]), "ctx", distance + offset))
        running = inner_block(running, query_heads, near_key, near_value, inner_flags(frame_step))
        running = outer_block(
            running,
            query_heads,
            jnp.stack([corners[0][0], corners[1][0]]),
            jnp.stack([corners[0][1], corners[1][1]]),
            outer_flags(frame_step),
        )
    run_max, run_sum, run_out = running
    finished = (run_out / run_sum[..., None]).astype(jnp.bfloat16)
    finished = finished.transpose(1, 0, 2).reshape(2 * tile_tok, head_count * HD)
    first_out = finished[:tile_tok]
    second_out = finished[tile_tok:]
    mine_out = jnp.where(pair_side == 0, first_out, second_out)
    partner_out = jnp.where(pair_side == 0, second_out, first_out)
    returned = swapped(partner_out, "ctx", 0)
    whole_tile = jnp.where(
        pair_side == 0,
        jnp.concatenate([mine_out, returned], axis=1),
        jnp.concatenate([returned, mine_out], axis=1),
    )
    return lax.all_to_all(whole_tile, "head", split_axis=0, concat_axis=1, tiled=True)


HEADS_A_CHUNK = 1
FAR_LAG = 3
ATTEND_LAG = 5
VMEM_LIMIT = 60 * 2**20
LOG2_E = 1.4426950408889634
MESH = pl.DeviceIdType.MESH
OWN, CORE, BESIDE, FAR, BESIDE_CORE, FAR_CORE = range(6)


def attend(query, keys, values, beside_ok, far_ok, rows):
    scale = HD ** (-0.5) * LOG2_E
    scores = lax.dot_general(
        query, keys, (((1,), (1,)), ((), ())), preferred_element_type=jnp.float32
    )
    halves = [scores[:, slot * rows : (slot + 1) * rows] for slot in range(6)]
    own = jnp.maximum(halves[OWN], halves[CORE])
    beside = jnp.maximum(halves[BESIDE], halves[BESIDE_CORE])
    far = jnp.maximum(halves[FAR], halves[FAR_CORE])
    row_max = jnp.maximum(
        own, jnp.maximum(jnp.where(beside_ok, beside, NEG_BIG), jnp.where(far_ok, far, NEG_BIG))
    ).max(-1, keepdims=True)
    beside_max = jnp.where(beside_ok, row_max, -NEG_BIG)
    far_max = jnp.where(far_ok, row_max, -NEG_BIG)
    tops = (row_max, row_max, beside_max, far_max, beside_max, far_max)
    weights = [jnp.exp2((half - top) * scale) for half, top in zip(halves, tops)]
    row_sum = sum(weights[1:], weights[0]).sum(-1, keepdims=True)
    weights_b = jnp.concatenate([w.astype(jnp.bfloat16) for w in weights], axis=1)
    mixed = jnp.dot(weights_b, values, preferred_element_type=jnp.float32)
    return (mixed / row_sum).astype(jnp.bfloat16)


def row_kernel(
    tiles, heads_a_chunk,
    query_in, key_in, value_in, keep_in, result,
    query, pairs, keep, load_sem, send_sem, core_sem, paired_sem, far_sem, relay_sem,
):
    rows = query_in.shape[0]
    chunks = query_in.shape[1] // (heads_a_chunk * HD)
    width = heads_a_chunk * HD
    clip, tile, core = lax.axis_index("clips"), lax.axis_index("ctx"), lax.axis_index("head")
    side = lax.rem(tile, 2)
    step = 2 - 4 * side
    to_far, from_far = tile + step, tile - step
    sends_far = jnp.logical_and(to_far >= 0, to_far < tiles)
    gets_far = jnp.logical_and(from_far >= 0, from_far < tiles)
    other_core = (clip, tile, 1 - core)
    paired = (clip, tile + 1 - 2 * side, core)
    beyond = (clip, jnp.where(sends_far, to_far, tile + 1 - 2 * side), core)
    behind = (clip, jnp.where(gets_far, from_far, tile + 1 - 2 * side), core)

    def place(slot, count=1):
        return pl.ds(slot * rows, count * rows)

    def columns(chunk):
        return pl.ds(pl.multiple_of(chunk * width, width), width)

    everything = slice(None)

    def own_copy(which, slot, device, at, sender, receiver):
        return pltpu.make_async_remote_copy(
            src_ref=(key_in, value_in)[which].at[:, at],
            dst_ref=pairs.at[which, place(slot), at],
            send_sem=send_sem.at[sender],
            recv_sem=receiver,
            device_id=device,
            device_id_type=MESH,
        )

    def relay(source, slot, count, device, at, sender, receiver):
        return pltpu.make_async_remote_copy(
            src_ref=pairs.at[:, place(source, count), at],
            dst_ref=pairs.at[:, place(slot, count), at],
            send_sem=send_sem.at[sender],
            recv_sem=receiver,
            device_id=device,
            device_id_type=MESH,
        )

    def to_far_tile(chunk):
        return relay(BESIDE, FAR, 1, beyond, columns(chunk), 2, far_sem.at[chunk])

    def to_other_core(chunk):
        return relay(BESIDE, BESIDE_CORE, 2, other_core, columns(chunk), 3, relay_sem.at[chunk])

    def both_arrived(slot, at, receiver):
        relay(slot, slot, 1, paired, at, 0, receiver).wait_recv()

    loads = (
        pltpu.make_async_copy(keep_in, keep, load_sem.at[3]),
        pltpu.make_async_copy(query_in, query, load_sem.at[0]),
        pltpu.make_async_copy(key_in, pairs.at[0, place(OWN)], load_sem.at[1]),
        pltpu.make_async_copy(value_in, pairs.at[1, place(OWN)], load_sem.at[2]),
    )

    barrier = pltpu.get_barrier_semaphore()
    pl.semaphore_signal(barrier, inc=1, device_id=paired, device_id_type=MESH)

    @pl.when(sends_far)
    def _():
        pl.semaphore_signal(barrier, inc=1, device_id=beyond, device_id_type=MESH)

    @pl.when(gets_far)
    def _():
        pl.semaphore_signal(barrier, inc=1, device_id=behind, device_id_type=MESH)

    pl.semaphore_signal(barrier, inc=1, device_id=other_core, device_id_type=MESH)

    for load in loads:
        load.start()

    @pl.when(jnp.logical_not(gets_far))
    def _():
        pairs[:, place(FAR), :] = jnp.zeros((2, rows, pairs.shape[2]), pairs.dtype)

    pl.semaphore_wait(
        barrier, 2 + sends_far.astype(jnp.int32) + gets_far.astype(jnp.int32)
    )

    @pl.loop(0, chunks)
    def _(chunk):
        for which in range(2):
            own_copy(which, BESIDE, paired, columns(chunk), 0, paired_sem.at[chunk]).start()

    for which in range(2):
        own_copy(which, CORE, other_core, everything, 1, core_sem).start()

    for load in loads:
        load.wait()
    beside_ok = jnp.where(side == 0, keep[0, 1, 2, 0, tile], keep[0, 1, 0, 0, tile]) > 0
    far_ok = jnp.logical_and(
        jnp.where(side == 0, keep[0, 1, 0, 0, tile], keep[0, 1, 2, 0, tile]) > 0, gets_far
    )
    both_arrived(CORE, everything, core_sem)

    @pl.loop(0, chunks + ATTEND_LAG)
    def _(turn):
        @pl.when(turn < chunks)
        def _():
            both_arrived(BESIDE, columns(turn), paired_sem.at[turn])

            @pl.when(sends_far)
            def _():
                to_far_tile(turn).start()

        @pl.when(jnp.logical_and(turn >= FAR_LAG, turn < chunks + FAR_LAG))
        def _():
            @pl.when(gets_far)
            def _():
                to_far_tile(turn - FAR_LAG).wait_recv()

            to_other_core(turn - FAR_LAG).start()

        @pl.when(turn >= ATTEND_LAG)
        def _():
            chunk = turn - ATTEND_LAG
            to_other_core(chunk).wait_recv()
            for head in range(heads_a_chunk):
                at = pl.ds(pl.multiple_of(chunk * width + head * HD, HD), HD)
                result[:, at] = attend(
                    query[:, at], pairs[0, :, at], pairs[1, :, at], beside_ok, far_ok, rows
                )

    relay(BESIDE, BESIDE, 1, paired, everything, 0, core_sem).wait_send()
    relay(BESIDE, BESIDE, 1, paired, everything, 1, core_sem).wait_send()
    relay(BESIDE, BESIDE, 2, paired, everything, 3, core_sem).wait_send()

    @pl.when(sends_far)
    def _():
        relay(BESIDE, BESIDE, 1, paired, everything, 2, core_sem).wait_send()


def one_row(query_in, key_in, value_in, block_keep):
    rows, width = query_in.shape
    heads = width // HD
    heads_a_chunk = HEADS_A_CHUNK
    chunks = heads // heads_a_chunk
    return pl.pallas_call(
        functools.partial(row_kernel, lax.axis_size("ctx"), heads_a_chunk),
        out_shape=pltpu.VMEM((rows, width), jnp.bfloat16),
        in_specs=[pl.BlockSpec(memory_space=pl.ANY)] * 4,
        out_specs=pl.BlockSpec(memory_space=pltpu.VMEM),
        scratch_shapes=[
            pltpu.VMEM((rows, width), jnp.bfloat16),
            pltpu.VMEM((2, 6 * rows, width), jnp.bfloat16),
            pltpu.SMEM((1, 3, 3) + block_keep.shape[1:3], jnp.int32),
            pltpu.SemaphoreType.DMA((4,)),
            pltpu.SemaphoreType.DMA((4,)),
            pltpu.SemaphoreType.DMA,
            pltpu.SemaphoreType.DMA((chunks,)),
            pltpu.SemaphoreType.DMA((chunks,)),
            pltpu.SemaphoreType.DMA((chunks,)),
        ],
        compiler_params=pltpu.CompilerParams(
            collective_id=0, has_side_effects=True, vmem_limit_bytes=VMEM_LIMIT
        ),
        cost_estimate=pl.CostEstimate(
            flops=24 * rows * rows * width,
            bytes_accessed=10 * rows * width,
            transcendentals=6 * rows * rows * heads,
        ),
    )(query_in, key_in, value_in, block_keep.transpose(0, 3, 4, 1, 2))


def solution(mesh):
    in_one_row = mesh.shape["ctx"] == COLS // TILE_S
    return jax.shard_map(
        one_row if in_one_row else local,
        mesh=mesh,
        in_specs=(
            P(("clips", "ctx", "head"), None),
            P(("clips", "ctx", "head"), None),
            P(("clips", "ctx", "head"), None),
            P("clips", None, None, None, None),
        ),
        out_specs=P(("clips", "ctx", "head"), None),
        check_vma=False,
    )
```

```python
import functools

import jax
import jax.numpy as jnp
from jax import lax
from jax.experimental import pallas as pl
from jax.experimental.pallas import tpu as pltpu
from jax.sharding import PartitionSpec as P

HD = 128
TILE_S = 8
COLS = 64


NEG_BIG = -1e30


def swapped(block, axis, distance):
    count = lax.axis_size(axis)
    route = []
    for low in range(count):
        high = low | 1 << distance
        if high != low and high < count:
            route += [(low, high), (high, low)]
    return lax.ppermute(block, axis, route)


def from_behind(block, axis, distance):
    devices = range(lax.axis_size(axis))
    route = [(i - distance, i) for i in devices if i - distance in devices]
    return lax.ppermute(block, axis, route)


def order_pair(pair_side, mine, partner):
    first = jnp.where(pair_side == 0, mine, partner)
    second = jnp.where(pair_side == 0, partner, mine)
    return jnp.concatenate([first, second], axis=0)


def tile_flag(keep_pair, frame_at, col_at, frame_tiles, col_tiles, query_pos, frame_step, column):
    spot = column - query_pos + 1
    if frame_step == 1 and spot == 1:
        return jnp.array(True)
    frame_ok = (frame_at + frame_step - 1 >= 0) & (frame_at + frame_step - 1 < frame_tiles)
    col_ok = (col_at + column >= 0) & (col_at + column < col_tiles)
    return keep_pair[query_pos, frame_step, spot] & frame_ok & col_ok


def absorb(running, scores, allowed, mix_values):
    run_max, run_sum, run_out = running
    masked = jnp.where(allowed[None], scores, NEG_BIG)
    new_max = jnp.maximum(run_max, masked.max(-1))
    block_sum = jnp.where(allowed[None], jnp.exp(masked - new_max[..., None]), 0.0).sum(-1)
    weights_b = jnp.where(allowed[None], jnp.exp(masked - new_max[..., None]), 0.0).astype(
        jnp.bfloat16
    )
    factor = jnp.exp(run_max - new_max)
    new_sum = run_sum * factor + block_sum
    product = mix_values(weights_b)
    return (new_max, new_sum, run_out * factor[..., None] + product)


def inner_block(running, query_heads, key_pair, value_pair, tile_flags):
    tile_tok = key_pair.shape[0] // 2
    head_count = query_heads.shape[1]
    allowed = jnp.broadcast_to(tile_flags[:, None, :, None], (2, tile_tok, 2, tile_tok)).reshape(
        2 * tile_tok, 2 * tile_tok
    )
    key_rows = key_pair.reshape(2 * tile_tok, head_count, HD)
    value_rows = value_pair.reshape(2 * tile_tok, head_count, HD)
    scores = jnp.einsum(
        "qhd,khd->hqk", query_heads, key_rows, preferred_element_type=jnp.float32
    ) * HD ** (-0.5)

    def mix_values(weights_b):
        return jnp.einsum("hqk,khd->hqd", weights_b, value_rows, preferred_element_type=jnp.float32)

    return absorb(running, scores, allowed, mix_values)


def outer_block(running, query_heads, key_groups, value_groups, tile_flags):
    tile_tok = key_groups.shape[1]
    head_count = query_heads.shape[1]
    allowed = jnp.broadcast_to(tile_flags[:, None, None], (2, tile_tok, tile_tok)).reshape(
        2 * tile_tok, tile_tok
    )
    query_groups = query_heads.reshape(2, tile_tok, head_count, HD)
    key_rows = key_groups.reshape(2, tile_tok, head_count, HD)
    value_rows = value_groups.reshape(2, tile_tok, head_count, HD)
    scores = jnp.einsum(
        "gqhd,gkhd->hgqk", query_groups, key_rows, preferred_element_type=jnp.float32
    ) * HD ** (-0.5)
    scores = scores.reshape(head_count, 2 * tile_tok, tile_tok)

    def mix_values(weights_b):
        grouped = weights_b.reshape(head_count, 2, tile_tok, tile_tok)
        mixed = jnp.einsum(
            "hgqk,gkhd->hgqd", grouped, value_rows, preferred_element_type=jnp.float32
        )
        return mixed.reshape(head_count, 2 * tile_tok, HD)

    return absorb(running, scores, allowed, mix_values)


def local(query_in, key_in, value_in, block_keep):
    ctx_count = lax.axis_size("ctx")
    ctx_place = lax.axis_index("ctx")
    col_tiles = COLS // TILE_S
    row_tiles = max(1, ctx_count // (4 * col_tiles))
    frame_tiles = ctx_count // (row_tiles * col_tiles)
    frame_stride = row_tiles * col_tiles
    query_full, key_full, value_full = (
        lax.all_to_all(query_in, "head", split_axis=1, concat_axis=0, tiled=True),
        lax.all_to_all(key_in, "head", split_axis=1, concat_axis=0, tiled=True),
        lax.all_to_all(value_in, "head", split_axis=1, concat_axis=0, tiled=True),
    )
    tile_tok = query_full.shape[0]
    half_width = query_full.shape[1] // 2
    head_count = half_width // HD
    pair_side = ctx_place % 2

    def part_of(array, which):
        return lax.dynamic_slice_in_dim(array, which * half_width, half_width, 1)

    other_side = 1 - pair_side
    got_query, got_key, got_value = swapped(
        (
            part_of(query_full, other_side),
            part_of(key_full, other_side),
            part_of(value_full, other_side),
        ),
        "ctx",
        0,
    )
    query_pair = order_pair(pair_side, part_of(query_full, pair_side), got_query)
    key_pair = order_pair(pair_side, part_of(key_full, pair_side), got_key)
    value_pair = order_pair(pair_side, part_of(value_full, pair_side), got_value)
    query_heads = query_pair.reshape(2 * tile_tok, head_count, HD)
    first_tile = ctx_place - pair_side
    frame_at = first_tile // frame_stride
    col_at = first_tile % col_tiles
    keep_all = (block_keep > 0).reshape(-1, 3, 3)
    keep_pair = lax.dynamic_slice_in_dim(keep_all, first_tile, 2, 0)

    def inner_flags(frame_step):
        rows_list = []
        for query_pos in (0, 1):
            rows_list.append(
                jnp.stack(
                    [
                        tile_flag(
                            keep_pair,
                            frame_at,
                            col_at,
                            frame_tiles,
                            col_tiles,
                            query_pos,
                            frame_step,
                            column,
                        )
                        for column in (0, 1)
                    ]
                )
            )
        return jnp.stack(rows_list)

    def outer_flags(frame_step):
        left_flag = tile_flag(
            keep_pair, frame_at, col_at, frame_tiles, col_tiles, 0, frame_step, -1
        )
        right_flag = tile_flag(
            keep_pair, frame_at, col_at, frame_tiles, col_tiles, 1, frame_step, 2
        )
        return jnp.stack([left_flag, right_flag])

    side_tiles = []
    for distance, which_tile in ((2, 1), (-2, 0)):
        sent_tile = (
            key_pair[which_tile * tile_tok : (which_tile + 1) * tile_tok],
            value_pair[which_tile * tile_tok : (which_tile + 1) * tile_tok],
        )
        side_tiles.append(from_behind((sent_tile[0], sent_tile[1]), "ctx", distance))
    left_tile, right_tile = side_tiles
    running = (
        jnp.full((head_count, 2 * tile_tok), NEG_BIG, jnp.float32),
        jnp.zeros((head_count, 2 * tile_tok), jnp.float32),
        jnp.zeros((head_count, 2 * tile_tok, HD), jnp.float32),
    )
    running = inner_block(running, query_heads, key_pair, value_pair, inner_flags(1))
    running = outer_block(
        running,
        query_heads,
        jnp.stack([left_tile[0], right_tile[0]]),
        jnp.stack([left_tile[1], right_tile[1]]),
        outer_flags(1),
    )
    for frame_step, distance in ((0, frame_stride), (2, -frame_stride)):
        near_key, near_value = from_behind((key_pair, value_pair), "ctx", distance)
        corners = []
        for offset, which_tile in ((2, 1), (-2, 0)):
            sent_tile = (
                key_pair[which_tile * tile_tok : (which_tile + 1) * tile_tok],
                value_pair[which_tile * tile_tok : (which_tile + 1) * tile_tok],
            )
            corners.append(from_behind((sent_tile[0], sent_tile[1]), "ctx", distance + offset))
        running = inner_block(running, query_heads, near_key, near_value, inner_flags(frame_step))
        running = outer_block(
            running,
            query_heads,
            jnp.stack([corners[0][0], corners[1][0]]),
            jnp.stack([corners[0][1], corners[1][1]]),
            outer_flags(frame_step),
        )
    run_max, run_sum, run_out = running
    finished = (run_out / run_sum[..., None]).astype(jnp.bfloat16)
    finished = finished.transpose(1, 0, 2).reshape(2 * tile_tok, head_count * HD)
    first_out = finished[:tile_tok]
    second_out = finished[tile_tok:]
    mine_out = jnp.where(pair_side == 0, first_out, second_out)
    partner_out = jnp.where(pair_side == 0, second_out, first_out)
    returned = swapped(partner_out, "ctx", 0)
    whole_tile = jnp.where(
        pair_side == 0,
        jnp.concatenate([mine_out, returned], axis=1),
        jnp.concatenate([returned, mine_out], axis=1),
    )
    return lax.all_to_all(whole_tile, "head", split_axis=0, concat_axis=1, tiled=True)


HEADS_A_CHUNK = 1
FAR_LAG = 3
ATTEND_LAG = 5
VMEM_LIMIT = 60 * 2**20
LOG2_E = 1.4426950408889634
MESH = pl.DeviceIdType.MESH
OWN, CORE, BESIDE, FAR, BESIDE_CORE, FAR_CORE = range(6)


def attend(query, keys, values, beside_ok, far_ok, rows):
    scale = HD ** (-0.5) * LOG2_E
    scores = lax.dot_general(
        query, keys, (((1,), (1,)), ((), ())), preferred_element_type=jnp.float32
    )
    halves = [scores[:, slot * rows : (slot + 1) * rows] for slot in range(6)]
    own = jnp.maximum(halves[OWN], halves[CORE])
    beside = jnp.maximum(halves[BESIDE], halves[BESIDE_CORE])
    far = jnp.maximum(halves[FAR], halves[FAR_CORE])
    row_max = jnp.maximum(
        own, jnp.maximum(jnp.where(beside_ok, beside, NEG_BIG), jnp.where(far_ok, far, NEG_BIG))
    ).max(-1, keepdims=True)
    beside_max = jnp.where(beside_ok, row_max, -NEG_BIG)
    far_max = jnp.where(far_ok, row_max, -NEG_BIG)
    tops = (row_max, row_max, beside_max, far_max, beside_max, far_max)
    weights = [jnp.exp2((half - top) * scale) for half, top in zip(halves, tops)]
    row_sum = sum(weights[1:], weights[0]).sum(-1, keepdims=True)
    weights_b = jnp.concatenate([w.astype(jnp.bfloat16) for w in weights], axis=1)
    mixed = jnp.dot(weights_b, values, preferred_element_type=jnp.float32)
    return (mixed / row_sum).astype(jnp.bfloat16)


def row_kernel(
    tiles, heads_a_chunk,
    query_in, key_in, value_in, keep_in, result,
    query, pairs, keep, load_sem, send_sem, core_sem, paired_sem, far_sem, relay_sem,
):
    rows = query_in.shape[0]
    chunks = query_in.shape[1] // (heads_a_chunk * HD)
    width = heads_a_chunk * HD
    clip, tile, core = lax.axis_index("clips"), lax.axis_index("ctx"), lax.axis_index("head")
    side = lax.rem(tile, 2)
    step = 2 - 4 * side
    to_far, from_far = tile + step, tile - step
    sends_far = jnp.logical_and(to_far >= 0, to_far < tiles)
    gets_far = jnp.logical_and(from_far >= 0, from_far < tiles)
    other_core = (clip, tile, 1 - core)
    paired = (clip, tile + 1 - 2 * side, core)
    beyond = (clip, jnp.where(sends_far, to_far, tile + 1 - 2 * side), core)
    behind = (clip, jnp.where(gets_far, from_far, tile + 1 - 2 * side), core)

    def place(slot, count=1):
        return pl.ds(slot * rows, count * rows)

    def columns(chunk):
        return pl.ds(pl.multiple_of(chunk * width, width), width)

    everything = slice(None)

    def own_copy(which, slot, device, at, sender, receiver):
        return pltpu.make_async_remote_copy(
            src_ref=(key_in, value_in)[which].at[:, at],
            dst_ref=pairs.at[which, place(slot), at],
            send_sem=send_sem.at[sender],
            recv_sem=receiver,
            device_id=device,
            device_id_type=MESH,
        )

    def relay(source, slot, count, device, at, sender, receiver, which=everything):
        return pltpu.make_async_remote_copy(
            src_ref=pairs.at[which, place(source, count), at],
            dst_ref=pairs.at[which, place(slot, count), at],
            send_sem=send_sem.at[sender],
            recv_sem=receiver,
            device_id=device,
            device_id_type=MESH,
        )

    def to_far_tile(chunk, which=everything):
        return relay(BESIDE, FAR, 1, beyond, columns(chunk), 2, far_sem.at[chunk], which)

    def to_other_core(chunk):
        return relay(BESIDE, BESIDE_CORE, 2, other_core, columns(chunk), 3, relay_sem.at[chunk])

    def both_arrived(slot, at, receiver):
        relay(slot, slot, 1, paired, at, 0, receiver).wait_recv()

    loads = (
        pltpu.make_async_copy(keep_in, keep, load_sem.at[3]),
        pltpu.make_async_copy(query_in, query, load_sem.at[0]),
        pltpu.make_async_copy(key_in, pairs.at[0, place(OWN)], load_sem.at[1]),
        pltpu.make_async_copy(value_in, pairs.at[1, place(OWN)], load_sem.at[2]),
    )

    barrier = pltpu.get_barrier_semaphore()
    pl.semaphore_signal(barrier, inc=1, device_id=paired, device_id_type=MESH)

    @pl.when(sends_far)
    def _():
        pl.semaphore_signal(barrier, inc=1, device_id=beyond, device_id_type=MESH)

    @pl.when(gets_far)
    def _():
        pl.semaphore_signal(barrier, inc=1, device_id=behind, device_id_type=MESH)

    pl.semaphore_signal(barrier, inc=1, device_id=other_core, device_id_type=MESH)

    for load in loads:
        load.start()

    @pl.when(jnp.logical_not(gets_far))
    def _():
        pairs[:, place(FAR), :] = jnp.zeros((2, rows, pairs.shape[2]), pairs.dtype)

    pl.semaphore_wait(
        barrier, 2 + sends_far.astype(jnp.int32) + gets_far.astype(jnp.int32)
    )

    @pl.loop(0, chunks)
    def _(chunk):
        for which in range(2):
            own_copy(which, BESIDE, paired, columns(chunk), 0, paired_sem.at[which, chunk]).start()

    for which in range(2):
        own_copy(which, CORE, other_core, everything, 1, core_sem).start()

    loads[0].wait()
    beside_ok = jnp.where(side == 0, keep[0, 1, 2, 0, tile], keep[0, 1, 0, 0, tile]) > 0
    far_ok = jnp.logical_and(
        jnp.where(side == 0, keep[0, 1, 0, 0, tile], keep[0, 1, 2, 0, tile]) > 0, gets_far
    )
    @pl.loop(0, chunks + ATTEND_LAG)
    def _(turn):
        @pl.when(turn < chunks)
        def _():
            for which in range(2):
                own_copy(
                    which, BESIDE, paired, columns(turn), 0, paired_sem.at[which, turn]
                ).wait_recv()

                @pl.when(sends_far)
                def _():
                    to_far_tile(turn, which).start()

        @pl.when(jnp.logical_and(turn >= FAR_LAG, turn < chunks + FAR_LAG))
        def _():
            @pl.when(gets_far)
            def _():
                to_far_tile(turn - FAR_LAG).wait_recv()

            to_other_core(turn - FAR_LAG).start()

        @pl.when(turn == ATTEND_LAG)
        def _():
            for load in loads[1:]:
                load.wait()
            both_arrived(CORE, everything, core_sem)

        @pl.when(turn >= ATTEND_LAG)
        def _():
            chunk = turn - ATTEND_LAG
            to_other_core(chunk).wait_recv()
            for head in range(heads_a_chunk):
                at = pl.ds(pl.multiple_of(chunk * width + head * HD, HD), HD)
                result[:, at] = attend(
                    query[:, at], pairs[0, :, at], pairs[1, :, at], beside_ok, far_ok, rows
                )

    relay(BESIDE, BESIDE, 1, paired, everything, 0, core_sem).wait_send()
    relay(BESIDE, BESIDE, 1, paired, everything, 1, core_sem).wait_send()
    relay(BESIDE, BESIDE, 2, paired, everything, 3, core_sem).wait_send()

    @pl.when(sends_far)
    def _():
        relay(BESIDE, BESIDE, 1, paired, everything, 2, core_sem).wait_send()


def one_row(query_in, key_in, value_in, block_keep):
    rows, width = query_in.shape
    heads = width // HD
    heads_a_chunk = HEADS_A_CHUNK
    chunks = heads // heads_a_chunk
    return pl.pallas_call(
        functools.partial(row_kernel, lax.axis_size("ctx"), heads_a_chunk),
        out_shape=pltpu.VMEM((rows, width), jnp.bfloat16),
        in_specs=[pl.BlockSpec(memory_space=pl.ANY)] * 4,
        out_specs=pl.BlockSpec(memory_space=pltpu.VMEM),
        scratch_shapes=[
            pltpu.VMEM((rows, width), jnp.bfloat16),
            pltpu.VMEM((2, 6 * rows, width), jnp.bfloat16),
            pltpu.SMEM((1, 3, 3) + block_keep.shape[1:3], jnp.int32),
            pltpu.SemaphoreType.DMA((4,)),
            pltpu.SemaphoreType.DMA((4,)),
            pltpu.SemaphoreType.DMA,
            pltpu.SemaphoreType.DMA((2, chunks)),
            pltpu.SemaphoreType.DMA((chunks,)),
            pltpu.SemaphoreType.DMA((chunks,)),
        ],
        compiler_params=pltpu.CompilerParams(
            collective_id=0, has_side_effects=True, vmem_limit_bytes=VMEM_LIMIT
        ),
        cost_estimate=pl.CostEstimate(
            flops=24 * rows * rows * width,
            bytes_accessed=10 * rows * width,
            transcendentals=6 * rows * rows * heads,
        ),
    )(query_in, key_in, value_in, block_keep.transpose(0, 3, 4, 1, 2))


def solution(mesh):
    in_one_row = mesh.shape["ctx"] == COLS // TILE_S
    return jax.shard_map(
        one_row if in_one_row else local,
        mesh=mesh,
        in_specs=(
            P(("clips", "ctx", "head"), None),
            P(("clips", "ctx", "head"), None),
            P(("clips", "ctx", "head"), None),
            P("clips", None, None, None, None),
        ),
        out_specs=P(("clips", "ctx", "head"), None),
        check_vma=False,
    )
```

```python
import functools

import jax
import jax.numpy as jnp
from jax import lax
from jax.experimental import pallas as pl
from jax.experimental.pallas import tpu as pltpu
from jax.sharding import PartitionSpec as P

HD = 128
TILE_S = 8
COLS = 64


NEG_BIG = -1e30


def swapped(block, axis, distance):
    count = lax.axis_size(axis)
    route = []
    for low in range(count):
        high = low | 1 << distance
        if high != low and high < count:
            route += [(low, high), (high, low)]
    return lax.ppermute(block, axis, route)


def from_behind(block, axis, distance):
    devices = range(lax.axis_size(axis))
    route = [(i - distance, i) for i in devices if i - distance in devices]
    return lax.ppermute(block, axis, route)


def order_pair(pair_side, mine, partner):
    first = jnp.where(pair_side == 0, mine, partner)
    second = jnp.where(pair_side == 0, partner, mine)
    return jnp.concatenate([first, second], axis=0)


def tile_flag(keep_pair, frame_at, col_at, frame_tiles, col_tiles, query_pos, frame_step, column):
    spot = column - query_pos + 1
    if frame_step == 1 and spot == 1:
        return jnp.array(True)
    frame_ok = (frame_at + frame_step - 1 >= 0) & (frame_at + frame_step - 1 < frame_tiles)
    col_ok = (col_at + column >= 0) & (col_at + column < col_tiles)
    return keep_pair[query_pos, frame_step, spot] & frame_ok & col_ok


def absorb(running, scores, allowed, mix_values):
    run_max, run_sum, run_out = running
    masked = jnp.where(allowed[None], scores, NEG_BIG)
    new_max = jnp.maximum(run_max, masked.max(-1))
    block_sum = jnp.where(allowed[None], jnp.exp(masked - new_max[..., None]), 0.0).sum(-1)
    weights_b = jnp.where(allowed[None], jnp.exp(masked - new_max[..., None]), 0.0).astype(
        jnp.bfloat16
    )
    factor = jnp.exp(run_max - new_max)
    new_sum = run_sum * factor + block_sum
    product = mix_values(weights_b)
    return (new_max, new_sum, run_out * factor[..., None] + product)


def inner_block(running, query_heads, key_pair, value_pair, tile_flags):
    tile_tok = key_pair.shape[0] // 2
    head_count = query_heads.shape[1]
    allowed = jnp.broadcast_to(tile_flags[:, None, :, None], (2, tile_tok, 2, tile_tok)).reshape(
        2 * tile_tok, 2 * tile_tok
    )
    key_rows = key_pair.reshape(2 * tile_tok, head_count, HD)
    value_rows = value_pair.reshape(2 * tile_tok, head_count, HD)
    scores = jnp.einsum(
        "qhd,khd->hqk", query_heads, key_rows, preferred_element_type=jnp.float32
    ) * HD ** (-0.5)

    def mix_values(weights_b):
        return jnp.einsum("hqk,khd->hqd", weights_b, value_rows, preferred_element_type=jnp.float32)

    return absorb(running, scores, allowed, mix_values)


def outer_block(running, query_heads, key_groups, value_groups, tile_flags):
    tile_tok = key_groups.shape[1]
    head_count = query_heads.shape[1]
    allowed = jnp.broadcast_to(tile_flags[:, None, None], (2, tile_tok, tile_tok)).reshape(
        2 * tile_tok, tile_tok
    )
    query_groups = query_heads.reshape(2, tile_tok, head_count, HD)
    key_rows = key_groups.reshape(2, tile_tok, head_count, HD)
    value_rows = value_groups.reshape(2, tile_tok, head_count, HD)
    scores = jnp.einsum(
        "gqhd,gkhd->hgqk", query_groups, key_rows, preferred_element_type=jnp.float32
    ) * HD ** (-0.5)
    scores = scores.reshape(head_count, 2 * tile_tok, tile_tok)

    def mix_values(weights_b):
        grouped = weights_b.reshape(head_count, 2, tile_tok, tile_tok)
        mixed = jnp.einsum(
            "hgqk,gkhd->hgqd", grouped, value_rows, preferred_element_type=jnp.float32
        )
        return mixed.reshape(head_count, 2 * tile_tok, HD)

    return absorb(running, scores, allowed, mix_values)


def local(query_in, key_in, value_in, block_keep):
    ctx_count = lax.axis_size("ctx")
    ctx_place = lax.axis_index("ctx")
    col_tiles = COLS // TILE_S
    row_tiles = max(1, ctx_count // (4 * col_tiles))
    frame_tiles = ctx_count // (row_tiles * col_tiles)
    frame_stride = row_tiles * col_tiles
    query_full, key_full, value_full = (
        lax.all_to_all(query_in, "head", split_axis=1, concat_axis=0, tiled=True),
        lax.all_to_all(key_in, "head", split_axis=1, concat_axis=0, tiled=True),
        lax.all_to_all(value_in, "head", split_axis=1, concat_axis=0, tiled=True),
    )
    tile_tok = query_full.shape[0]
    half_width = query_full.shape[1] // 2
    head_count = half_width // HD
    pair_side = ctx_place % 2

    def part_of(array, which):
        return lax.dynamic_slice_in_dim(array, which * half_width, half_width, 1)

    other_side = 1 - pair_side
    got_query, got_key, got_value = swapped(
        (
            part_of(query_full, other_side),
            part_of(key_full, other_side),
            part_of(value_full, other_side),
        ),
        "ctx",
        0,
    )
    query_pair = order_pair(pair_side, part_of(query_full, pair_side), got_query)
    key_pair = order_pair(pair_side, part_of(key_full, pair_side), got_key)
    value_pair = order_pair(pair_side, part_of(value_full, pair_side), got_value)
    query_heads = query_pair.reshape(2 * tile_tok, head_count, HD)
    first_tile = ctx_place - pair_side
    frame_at = first_tile // frame_stride
    col_at = first_tile % col_tiles
    keep_all = (block_keep > 0).reshape(-1, 3, 3)
    keep_pair = lax.dynamic_slice_in_dim(keep_all, first_tile, 2, 0)

    def inner_flags(frame_step):
        rows_list = []
        for query_pos in (0, 1):
            rows_list.append(
                jnp.stack(
                    [
                        tile_flag(
                            keep_pair,
                            frame_at,
                            col_at,
                            frame_tiles,
                            col_tiles,
                            query_pos,
                            frame_step,
                            column,
                        )
                        for column in (0, 1)
                    ]
                )
            )
        return jnp.stack(rows_list)

    def outer_flags(frame_step):
        left_flag = tile_flag(
            keep_pair, frame_at, col_at, frame_tiles, col_tiles, 0, frame_step, -1
        )
        right_flag = tile_flag(
            keep_pair, frame_at, col_at, frame_tiles, col_tiles, 1, frame_step, 2
        )
        return jnp.stack([left_flag, right_flag])

    side_tiles = []
    for distance, which_tile in ((2, 1), (-2, 0)):
        sent_tile = (
            key_pair[which_tile * tile_tok : (which_tile + 1) * tile_tok],
            value_pair[which_tile * tile_tok : (which_tile + 1) * tile_tok],
        )
        side_tiles.append(from_behind((sent_tile[0], sent_tile[1]), "ctx", distance))
    left_tile, right_tile = side_tiles
    running = (
        jnp.full((head_count, 2 * tile_tok), NEG_BIG, jnp.float32),
        jnp.zeros((head_count, 2 * tile_tok), jnp.float32),
        jnp.zeros((head_count, 2 * tile_tok, HD), jnp.float32),
    )
    running = inner_block(running, query_heads, key_pair, value_pair, inner_flags(1))
    running = outer_block(
        running,
        query_heads,
        jnp.stack([left_tile[0], right_tile[0]]),
        jnp.stack([left_tile[1], right_tile[1]]),
        outer_flags(1),
    )
    for frame_step, distance in ((0, frame_stride), (2, -frame_stride)):
        near_key, near_value = from_behind((key_pair, value_pair), "ctx", distance)
        corners = []
        for offset, which_tile in ((2, 1), (-2, 0)):
            sent_tile = (
                key_pair[which_tile * tile_tok : (which_tile + 1) * tile_tok],
                value_pair[which_tile * tile_tok : (which_tile + 1) * tile_tok],
            )
            corners.append(from_behind((sent_tile[0], sent_tile[1]), "ctx", distance + offset))
        running = inner_block(running, query_heads, near_key, near_value, inner_flags(frame_step))
        running = outer_block(
            running,
            query_heads,
            jnp.stack([corners[0][0], corners[1][0]]),
            jnp.stack([corners[0][1], corners[1][1]]),
            outer_flags(frame_step),
        )
    run_max, run_sum, run_out = running
    finished = (run_out / run_sum[..., None]).astype(jnp.bfloat16)
    finished = finished.transpose(1, 0, 2).reshape(2 * tile_tok, head_count * HD)
    first_out = finished[:tile_tok]
    second_out = finished[tile_tok:]
    mine_out = jnp.where(pair_side == 0, first_out, second_out)
    partner_out = jnp.where(pair_side == 0, second_out, first_out)
    returned = swapped(partner_out, "ctx", 0)
    whole_tile = jnp.where(
        pair_side == 0,
        jnp.concatenate([mine_out, returned], axis=1),
        jnp.concatenate([returned, mine_out], axis=1),
    )
    return lax.all_to_all(whole_tile, "head", split_axis=0, concat_axis=1, tiled=True)


HEADS_A_CHUNK = 1
FAR_LAG = 3
ATTEND_LAG = 5
VMEM_LIMIT = 60 * 2**20
LOG2_E = 1.4426950408889634
MESH = pl.DeviceIdType.MESH
OWN, CORE, BESIDE, FAR, BESIDE_CORE, FAR_CORE = range(6)


def attend(query, keys, values, beside_ok, far_ok, rows):
    scale = HD ** (-0.5) * LOG2_E
    scores = lax.dot_general(
        query, keys, (((1,), (1,)), ((), ())), preferred_element_type=jnp.float32
    )
    halves = [scores[:, slot * rows : (slot + 1) * rows] for slot in range(6)]
    own = jnp.maximum(halves[OWN], halves[CORE])
    beside = jnp.maximum(halves[BESIDE], halves[BESIDE_CORE])
    far = jnp.maximum(halves[FAR], halves[FAR_CORE])
    row_max = jnp.maximum(
        own, jnp.maximum(jnp.where(beside_ok, beside, NEG_BIG), jnp.where(far_ok, far, NEG_BIG))
    ).max(-1, keepdims=True)
    beside_max = jnp.where(beside_ok, row_max, -NEG_BIG)
    far_max = jnp.where(far_ok, row_max, -NEG_BIG)
    tops = (row_max, row_max, beside_max, far_max, beside_max, far_max)
    weights = [jnp.exp2((half - top) * scale) for half, top in zip(halves, tops)]
    row_sum = sum(weights[1:], weights[0]).sum(-1, keepdims=True)
    weights_b = jnp.concatenate([w.astype(jnp.bfloat16) for w in weights], axis=1)
    mixed = jnp.dot(weights_b, values, preferred_element_type=jnp.float32)
    return (mixed / row_sum).astype(jnp.bfloat16)


def row_kernel(
    tiles, heads_a_chunk,
    query_in, key_in, value_in, keep_in, result,
    query, pairs, keep, load_sem, send_sem, core_sem, paired_sem, far_sem, relay_sem,
):
    rows = query_in.shape[0]
    chunks = query_in.shape[1] // (heads_a_chunk * HD)
    width = heads_a_chunk * HD
    clip, tile, core = lax.axis_index("clips"), lax.axis_index("ctx"), lax.axis_index("head")
    side = lax.rem(tile, 2)
    step = 2 - 4 * side
    to_far, from_far = tile + step, tile - step
    sends_far = jnp.logical_and(to_far >= 0, to_far < tiles)
    gets_far = jnp.logical_and(from_far >= 0, from_far < tiles)
    other_core = (clip, tile, 1 - core)
    paired = (clip, tile + 1 - 2 * side, core)
    beyond = (clip, jnp.where(sends_far, to_far, tile + 1 - 2 * side), core)
    behind = (clip, jnp.where(gets_far, from_far, tile + 1 - 2 * side), core)

    def place(slot, count=1):
        return pl.ds(slot * rows, count * rows)

    def columns(chunk):
        return pl.ds(pl.multiple_of(chunk * width, width), width)

    everything = slice(None)

    def own_copy(which, slot, device, at, sender, receiver):
        return pltpu.make_async_remote_copy(
            src_ref=(key_in, value_in)[which].at[:, at],
            dst_ref=pairs.at[which, place(slot), at],
            send_sem=send_sem.at[sender],
            recv_sem=receiver,
            device_id=device,
            device_id_type=MESH,
        )

    def relay(source, slot, count, device, at, sender, receiver, which=everything):
        return pltpu.make_async_remote_copy(
            src_ref=pairs.at[which, place(source, count), at],
            dst_ref=pairs.at[which, place(slot, count), at],
            send_sem=send_sem.at[sender],
            recv_sem=receiver,
            device_id=device,
            device_id_type=MESH,
        )

    def to_far_tile(chunk, which=everything):
        return relay(BESIDE, FAR, 1, beyond, columns(chunk), 2, far_sem.at[chunk], which)

    def to_other_core(chunk, slot, count=1):
        return relay(
            slot, slot + 2, count, other_core, columns(chunk), 3, relay_sem.at[chunk]
        )

    def both_arrived(slot, at, receiver):
        relay(slot, slot, 1, paired, at, 0, receiver).wait_recv()

    loads = (
        pltpu.make_async_copy(keep_in, keep, load_sem.at[3]),
        pltpu.make_async_copy(query_in, query, load_sem.at[0]),
        pltpu.make_async_copy(key_in, pairs.at[0, place(OWN)], load_sem.at[1]),
        pltpu.make_async_copy(value_in, pairs.at[1, place(OWN)], load_sem.at[2]),
    )

    barrier = pltpu.get_barrier_semaphore()
    pl.semaphore_signal(barrier, inc=1, device_id=paired, device_id_type=MESH)

    @pl.when(sends_far)
    def _():
        pl.semaphore_signal(barrier, inc=1, device_id=beyond, device_id_type=MESH)

    @pl.when(gets_far)
    def _():
        pl.semaphore_signal(barrier, inc=1, device_id=behind, device_id_type=MESH)

    pl.semaphore_signal(barrier, inc=1, device_id=other_core, device_id_type=MESH)

    for load in loads:
        load.start()

    @pl.when(jnp.logical_not(gets_far))
    def _():
        pairs[:, place(FAR), :] = jnp.zeros((2, rows, pairs.shape[2]), pairs.dtype)

    pl.semaphore_wait(
        barrier, 2 + sends_far.astype(jnp.int32) + gets_far.astype(jnp.int32)
    )

    @pl.loop(0, chunks)
    def _(chunk):
        for which in range(2):
            own_copy(which, BESIDE, paired, columns(chunk), 0, paired_sem.at[which, chunk]).start()

    for which in range(2):
        own_copy(which, CORE, other_core, everything, 1, core_sem).start()

    loads[0].wait()
    beside_ok = jnp.where(side == 0, keep[0, 1, 2, 0, tile], keep[0, 1, 0, 0, tile]) > 0
    far_ok = jnp.logical_and(
        jnp.where(side == 0, keep[0, 1, 0, 0, tile], keep[0, 1, 2, 0, tile]) > 0, gets_far
    )
    @pl.loop(0, chunks + ATTEND_LAG)
    def _(turn):
        @pl.when(turn < chunks)
        def _():
            for which in range(2):
                own_copy(
                    which, BESIDE, paired, columns(turn), 0, paired_sem.at[which, turn]
                ).wait_recv()

                @pl.when(sends_far)
                def _():
                    to_far_tile(turn, which).start()

            to_other_core(turn, BESIDE).start()

        @pl.when(jnp.logical_and(turn >= FAR_LAG, turn < chunks + FAR_LAG))
        def _():
            @pl.when(gets_far)
            def _():
                to_far_tile(turn - FAR_LAG).wait_recv()

            to_other_core(turn - FAR_LAG, FAR).start()

        @pl.when(turn == ATTEND_LAG)
        def _():
            for load in loads[1:]:
                load.wait()
            both_arrived(CORE, everything, core_sem)

        @pl.when(turn >= ATTEND_LAG)
        def _():
            chunk = turn - ATTEND_LAG
            to_other_core(chunk, BESIDE, 2).wait_recv()
            for head in range(heads_a_chunk):
                at = pl.ds(pl.multiple_of(chunk * width + head * HD, HD), HD)
                result[:, at] = attend(
                    query[:, at], pairs[0, :, at], pairs[1, :, at], beside_ok, far_ok, rows
                )

    relay(BESIDE, BESIDE, 1, paired, everything, 0, core_sem).wait_send()
    relay(BESIDE, BESIDE, 1, paired, everything, 1, core_sem).wait_send()
    relay(BESIDE, BESIDE, 2, paired, everything, 3, core_sem).wait_send()

    @pl.when(sends_far)
    def _():
        relay(BESIDE, BESIDE, 1, paired, everything, 2, core_sem).wait_send()


def one_row(query_in, key_in, value_in, block_keep):
    rows, width = query_in.shape
    heads = width // HD
    heads_a_chunk = HEADS_A_CHUNK
    chunks = heads // heads_a_chunk
    return pl.pallas_call(
        functools.partial(row_kernel, lax.axis_size("ctx"), heads_a_chunk),
        out_shape=pltpu.VMEM((rows, width), jnp.bfloat16),
        in_specs=[pl.BlockSpec(memory_space=pl.ANY)] * 4,
        out_specs=pl.BlockSpec(memory_space=pltpu.VMEM),
        scratch_shapes=[
            pltpu.VMEM((rows, width), jnp.bfloat16),
            pltpu.VMEM((2, 6 * rows, width), jnp.bfloat16),
            pltpu.SMEM((1, 3, 3) + block_keep.shape[1:3], jnp.int32),
            pltpu.SemaphoreType.DMA((4,)),
            pltpu.SemaphoreType.DMA((4,)),
            pltpu.SemaphoreType.DMA,
            pltpu.SemaphoreType.DMA((2, chunks)),
            pltpu.SemaphoreType.DMA((chunks,)),
            pltpu.SemaphoreType.DMA((chunks,)),
        ],
        compiler_params=pltpu.CompilerParams(
            collective_id=0, has_side_effects=True, vmem_limit_bytes=VMEM_LIMIT
        ),
        cost_estimate=pl.CostEstimate(
            flops=24 * rows * rows * width,
            bytes_accessed=10 * rows * width,
            transcendentals=6 * rows * rows * heads,
        ),
    )(query_in, key_in, value_in, block_keep.transpose(0, 3, 4, 1, 2))


def solution(mesh):
    in_one_row = mesh.shape["ctx"] == COLS // TILE_S
    return jax.shard_map(
        one_row if in_one_row else local,
        mesh=mesh,
        in_specs=(
            P(("clips", "ctx", "head"), None),
            P(("clips", "ctx", "head"), None),
            P(("clips", "ctx", "head"), None),
            P("clips", None, None, None, None),
        ),
        out_specs=P(("clips", "ctx", "head"), None),
        check_vma=False,
    )
```

```python
import functools

import jax
import jax.numpy as jnp
from jax import lax
from jax.experimental import pallas as pl
from jax.experimental.pallas import tpu as pltpu
from jax.sharding import PartitionSpec as P

HD = 128
TILE_S = 8
COLS = 64


NEG_BIG = -1e30


def swapped(block, axis, distance):
    count = lax.axis_size(axis)
    route = []
    for low in range(count):
        high = low | 1 << distance
        if high != low and high < count:
            route += [(low, high), (high, low)]
    return lax.ppermute(block, axis, route)


def from_behind(block, axis, distance):
    devices = range(lax.axis_size(axis))
    route = [(i - distance, i) for i in devices if i - distance in devices]
    return lax.ppermute(block, axis, route)


def order_pair(pair_side, mine, partner):
    first = jnp.where(pair_side == 0, mine, partner)
    second = jnp.where(pair_side == 0, partner, mine)
    return jnp.concatenate([first, second], axis=0)


def tile_flag(keep_pair, frame_at, col_at, frame_tiles, col_tiles, query_pos, frame_step, column):
    spot = column - query_pos + 1
    if frame_step == 1 and spot == 1:
        return jnp.array(True)
    frame_ok = (frame_at + frame_step - 1 >= 0) & (frame_at + frame_step - 1 < frame_tiles)
    col_ok = (col_at + column >= 0) & (col_at + column < col_tiles)
    return keep_pair[query_pos, frame_step, spot] & frame_ok & col_ok


def absorb(running, scores, allowed, mix_values):
    run_max, run_sum, run_out = running
    masked = jnp.where(allowed[None], scores, NEG_BIG)
    new_max = jnp.maximum(run_max, masked.max(-1))
    block_sum = jnp.where(allowed[None], jnp.exp(masked - new_max[..., None]), 0.0).sum(-1)
    weights_b = jnp.where(allowed[None], jnp.exp(masked - new_max[..., None]), 0.0).astype(
        jnp.bfloat16
    )
    factor = jnp.exp(run_max - new_max)
    new_sum = run_sum * factor + block_sum
    product = mix_values(weights_b)
    return (new_max, new_sum, run_out * factor[..., None] + product)


def inner_block(running, query_heads, key_pair, value_pair, tile_flags):
    tile_tok = key_pair.shape[0] // 2
    head_count = query_heads.shape[1]
    allowed = jnp.broadcast_to(tile_flags[:, None, :, None], (2, tile_tok, 2, tile_tok)).reshape(
        2 * tile_tok, 2 * tile_tok
    )
    key_rows = key_pair.reshape(2 * tile_tok, head_count, HD)
    value_rows = value_pair.reshape(2 * tile_tok, head_count, HD)
    scores = jnp.einsum(
        "qhd,khd->hqk", query_heads, key_rows, preferred_element_type=jnp.float32
    ) * HD ** (-0.5)

    def mix_values(weights_b):
        return jnp.einsum("hqk,khd->hqd", weights_b, value_rows, preferred_element_type=jnp.float32)

    return absorb(running, scores, allowed, mix_values)


def outer_block(running, query_heads, key_groups, value_groups, tile_flags):
    tile_tok = key_groups.shape[1]
    head_count = query_heads.shape[1]
    allowed = jnp.broadcast_to(tile_flags[:, None, None], (2, tile_tok, tile_tok)).reshape(
        2 * tile_tok, tile_tok
    )
    query_groups = query_heads.reshape(2, tile_tok, head_count, HD)
    key_rows = key_groups.reshape(2, tile_tok, head_count, HD)
    value_rows = value_groups.reshape(2, tile_tok, head_count, HD)
    scores = jnp.einsum(
        "gqhd,gkhd->hgqk", query_groups, key_rows, preferred_element_type=jnp.float32
    ) * HD ** (-0.5)
    scores = scores.reshape(head_count, 2 * tile_tok, tile_tok)

    def mix_values(weights_b):
        grouped = weights_b.reshape(head_count, 2, tile_tok, tile_tok)
        mixed = jnp.einsum(
            "hgqk,gkhd->hgqd", grouped, value_rows, preferred_element_type=jnp.float32
        )
        return mixed.reshape(head_count, 2 * tile_tok, HD)

    return absorb(running, scores, allowed, mix_values)


def local(query_in, key_in, value_in, block_keep):
    ctx_count = lax.axis_size("ctx")
    ctx_place = lax.axis_index("ctx")
    col_tiles = COLS // TILE_S
    row_tiles = max(1, ctx_count // (4 * col_tiles))
    frame_tiles = ctx_count // (row_tiles * col_tiles)
    frame_stride = row_tiles * col_tiles
    query_full, key_full, value_full = (
        lax.all_to_all(query_in, "head", split_axis=1, concat_axis=0, tiled=True),
        lax.all_to_all(key_in, "head", split_axis=1, concat_axis=0, tiled=True),
        lax.all_to_all(value_in, "head", split_axis=1, concat_axis=0, tiled=True),
    )
    tile_tok = query_full.shape[0]
    half_width = query_full.shape[1] // 2
    head_count = half_width // HD
    pair_side = ctx_place % 2

    def part_of(array, which):
        return lax.dynamic_slice_in_dim(array, which * half_width, half_width, 1)

    other_side = 1 - pair_side
    got_query, got_key, got_value = swapped(
        (
            part_of(query_full, other_side),
            part_of(key_full, other_side),
            part_of(value_full, other_side),
        ),
        "ctx",
        0,
    )
    query_pair = order_pair(pair_side, part_of(query_full, pair_side), got_query)
    key_pair = order_pair(pair_side, part_of(key_full, pair_side), got_key)
    value_pair = order_pair(pair_side, part_of(value_full, pair_side), got_value)
    query_heads = query_pair.reshape(2 * tile_tok, head_count, HD)
    first_tile = ctx_place - pair_side
    frame_at = first_tile // frame_stride
    col_at = first_tile % col_tiles
    keep_all = (block_keep > 0).reshape(-1, 3, 3)
    keep_pair = lax.dynamic_slice_in_dim(keep_all, first_tile, 2, 0)

    def inner_flags(frame_step):
        rows_list = []
        for query_pos in (0, 1):
            rows_list.append(
                jnp.stack(
                    [
                        tile_flag(
                            keep_pair,
                            frame_at,
                            col_at,
                            frame_tiles,
                            col_tiles,
                            query_pos,
                            frame_step,
                            column,
                        )
                        for column in (0, 1)
                    ]
                )
            )
        return jnp.stack(rows_list)

    def outer_flags(frame_step):
        left_flag = tile_flag(
            keep_pair, frame_at, col_at, frame_tiles, col_tiles, 0, frame_step, -1
        )
        right_flag = tile_flag(
            keep_pair, frame_at, col_at, frame_tiles, col_tiles, 1, frame_step, 2
        )
        return jnp.stack([left_flag, right_flag])

    side_tiles = []
    for distance, which_tile in ((2, 1), (-2, 0)):
        sent_tile = (
            key_pair[which_tile * tile_tok : (which_tile + 1) * tile_tok],
            value_pair[which_tile * tile_tok : (which_tile + 1) * tile_tok],
        )
        side_tiles.append(from_behind((sent_tile[0], sent_tile[1]), "ctx", distance))
    left_tile, right_tile = side_tiles
    running = (
        jnp.full((head_count, 2 * tile_tok), NEG_BIG, jnp.float32),
        jnp.zeros((head_count, 2 * tile_tok), jnp.float32),
        jnp.zeros((head_count, 2 * tile_tok, HD), jnp.float32),
    )
    running = inner_block(running, query_heads, key_pair, value_pair, inner_flags(1))
    running = outer_block(
        running,
        query_heads,
        jnp.stack([left_tile[0], right_tile[0]]),
        jnp.stack([left_tile[1], right_tile[1]]),
        outer_flags(1),
    )
    for frame_step, distance in ((0, frame_stride), (2, -frame_stride)):
        near_key, near_value = from_behind((key_pair, value_pair), "ctx", distance)
        corners = []
        for offset, which_tile in ((2, 1), (-2, 0)):
            sent_tile = (
                key_pair[which_tile * tile_tok : (which_tile + 1) * tile_tok],
                value_pair[which_tile * tile_tok : (which_tile + 1) * tile_tok],
            )
            corners.append(from_behind((sent_tile[0], sent_tile[1]), "ctx", distance + offset))
        running = inner_block(running, query_heads, near_key, near_value, inner_flags(frame_step))
        running = outer_block(
            running,
            query_heads,
            jnp.stack([corners[0][0], corners[1][0]]),
            jnp.stack([corners[0][1], corners[1][1]]),
            outer_flags(frame_step),
        )
    run_max, run_sum, run_out = running
    finished = (run_out / run_sum[..., None]).astype(jnp.bfloat16)
    finished = finished.transpose(1, 0, 2).reshape(2 * tile_tok, head_count * HD)
    first_out = finished[:tile_tok]
    second_out = finished[tile_tok:]
    mine_out = jnp.where(pair_side == 0, first_out, second_out)
    partner_out = jnp.where(pair_side == 0, second_out, first_out)
    returned = swapped(partner_out, "ctx", 0)
    whole_tile = jnp.where(
        pair_side == 0,
        jnp.concatenate([mine_out, returned], axis=1),
        jnp.concatenate([returned, mine_out], axis=1),
    )
    return lax.all_to_all(whole_tile, "head", split_axis=0, concat_axis=1, tiled=True)


HEADS_A_CHUNK = 1
FAR_LAG = 3
ATTEND_LAG = 5
VMEM_LIMIT = 60 * 2**20
LOG2_E = 1.4426950408889634
MESH = pl.DeviceIdType.MESH
OWN, CORE, BESIDE, FAR, BESIDE_CORE, FAR_CORE = range(6)


def attend(query, keys, values, beside_ok, far_ok, rows):
    scale = HD ** (-0.5) * LOG2_E
    scores = lax.dot_general(
        query, keys, (((1,), (1,)), ((), ())), preferred_element_type=jnp.float32
    )
    halves = [scores[:, slot * rows : (slot + 1) * rows] for slot in range(6)]
    own = jnp.maximum(halves[OWN], halves[CORE])
    beside = jnp.maximum(halves[BESIDE], halves[BESIDE_CORE])
    far = jnp.maximum(halves[FAR], halves[FAR_CORE])
    row_max = jnp.maximum(
        own, jnp.maximum(jnp.where(beside_ok, beside, NEG_BIG), jnp.where(far_ok, far, NEG_BIG))
    ).max(-1, keepdims=True)
    beside_max = jnp.where(beside_ok, row_max, -NEG_BIG)
    far_max = jnp.where(far_ok, row_max, -NEG_BIG)
    tops = (row_max, row_max, beside_max, far_max, beside_max, far_max)
    weights = [jnp.exp2((half - top) * scale) for half, top in zip(halves, tops)]
    row_sum = sum(weights[1:], weights[0]).sum(-1, keepdims=True)
    weights_b = jnp.concatenate([w.astype(jnp.bfloat16) for w in weights], axis=1)
    mixed = jnp.dot(weights_b, values, preferred_element_type=jnp.float32)
    return (mixed / row_sum).astype(jnp.bfloat16)


def row_kernel(
    tiles, heads_a_chunk,
    query_in, key_in, value_in, keep_in, result,
    query, pairs, keep, load_sem, send_sem, core_sem, paired_sem, far_sem, relay_sem,
):
    rows = query_in.shape[0]
    chunks = query_in.shape[1] // (heads_a_chunk * HD)
    width = heads_a_chunk * HD
    clip, tile, core = lax.axis_index("clips"), lax.axis_index("ctx"), lax.axis_index("head")
    side = lax.rem(tile, 2)
    step = 2 - 4 * side
    to_far, from_far = tile + step, tile - step
    sends_far = jnp.logical_and(to_far >= 0, to_far < tiles)
    gets_far = jnp.logical_and(from_far >= 0, from_far < tiles)
    other_core = (clip, tile, 1 - core)
    paired = (clip, tile + 1 - 2 * side, core)
    beyond = (clip, jnp.where(sends_far, to_far, tile + 1 - 2 * side), core)
    behind = (clip, jnp.where(gets_far, from_far, tile + 1 - 2 * side), core)

    def place(slot, count=1):
        return pl.ds(slot * rows, count * rows)

    def columns(chunk):
        return pl.ds(pl.multiple_of(chunk * width, width), width)

    everything = slice(None)

    def own_copy(which, slot, device, at, sender, receiver):
        return pltpu.make_async_remote_copy(
            src_ref=(key_in, value_in)[which].at[:, at],
            dst_ref=pairs.at[which, place(slot), at],
            send_sem=send_sem.at[sender],
            recv_sem=receiver,
            device_id=device,
            device_id_type=MESH,
        )

    def relay(source, slot, count, device, at, sender, receiver, which=everything):
        return pltpu.make_async_remote_copy(
            src_ref=pairs.at[which, place(source, count), at],
            dst_ref=pairs.at[which, place(slot, count), at],
            send_sem=send_sem.at[sender],
            recv_sem=receiver,
            device_id=device,
            device_id_type=MESH,
        )

    def to_far_tile(chunk, which=everything):
        return relay(BESIDE, FAR, 1, beyond, columns(chunk), 2, far_sem.at[chunk], which)

    def to_other_core(chunk, slot, count=1):
        return relay(
            slot, slot + 2, count, other_core, columns(chunk), 3, relay_sem.at[chunk]
        )

    def both_arrived(slot, at, receiver):
        relay(slot, slot, 1, paired, at, 0, receiver).wait_recv()

    loads = (
        pltpu.make_async_copy(keep_in, keep, load_sem.at[3]),
        pltpu.make_async_copy(query_in, query, load_sem.at[0]),
        pltpu.make_async_copy(key_in, pairs.at[0, place(OWN)], load_sem.at[1]),
        pltpu.make_async_copy(value_in, pairs.at[1, place(OWN)], load_sem.at[2]),
    )

    barrier = pltpu.get_barrier_semaphore()
    pl.semaphore_signal(barrier, inc=1, device_id=paired, device_id_type=MESH)

    @pl.when(sends_far)
    def _():
        pl.semaphore_signal(barrier, inc=1, device_id=beyond, device_id_type=MESH)

    @pl.when(gets_far)
    def _():
        pl.semaphore_signal(barrier, inc=1, device_id=behind, device_id_type=MESH)

    pl.semaphore_signal(barrier, inc=1, device_id=other_core, device_id_type=MESH)

    for load in loads:
        load.start()

    @pl.when(jnp.logical_not(gets_far))
    def _():
        pairs[:, place(FAR), :] = jnp.zeros((2, rows, pairs.shape[2]), pairs.dtype)

    pl.semaphore_wait(
        barrier, 2 + sends_far.astype(jnp.int32) + gets_far.astype(jnp.int32)
    )

    for which in range(2):
        own_copy(which, CORE, other_core, everything, 1, core_sem).start()

    @pl.loop(0, chunks)
    def _(chunk):
        for which in range(2):
            own_copy(which, BESIDE, paired, columns(chunk), 0, paired_sem.at[which, chunk]).start()

    loads[0].wait()
    beside_ok = jnp.where(side == 0, keep[0, 1, 2, 0, tile], keep[0, 1, 0, 0, tile]) > 0
    far_ok = jnp.logical_and(
        jnp.where(side == 0, keep[0, 1, 0, 0, tile], keep[0, 1, 2, 0, tile]) > 0, gets_far
    )
    @pl.loop(0, chunks + ATTEND_LAG)
    def _(turn):
        @pl.when(turn < chunks)
        def _():
            for which in range(2):
                own_copy(
                    which, BESIDE, paired, columns(turn), 0, paired_sem.at[which, turn]
                ).wait_recv()

                @pl.when(sends_far)
                def _():
                    to_far_tile(turn, which).start()

            to_other_core(turn, BESIDE).start()

        @pl.when(jnp.logical_and(turn >= FAR_LAG, turn < chunks + FAR_LAG))
        def _():
            @pl.when(gets_far)
            def _():
                to_far_tile(turn - FAR_LAG).wait_recv()

            to_other_core(turn - FAR_LAG, FAR).start()

        @pl.when(turn == ATTEND_LAG)
        def _():
            for load in loads[1:]:
                load.wait()
            both_arrived(CORE, everything, core_sem)

        @pl.when(turn >= ATTEND_LAG)
        def _():
            chunk = turn - ATTEND_LAG
            to_other_core(chunk, BESIDE, 2).wait_recv()
            for head in range(heads_a_chunk):
                at = pl.ds(pl.multiple_of(chunk * width + head * HD, HD), HD)
                result[:, at] = attend(
                    query[:, at], pairs[0, :, at], pairs[1, :, at], beside_ok, far_ok, rows
                )

    relay(BESIDE, BESIDE, 1, paired, everything, 0, core_sem).wait_send()
    relay(BESIDE, BESIDE, 1, paired, everything, 1, core_sem).wait_send()
    relay(BESIDE, BESIDE, 2, paired, everything, 3, core_sem).wait_send()

    @pl.when(sends_far)
    def _():
        relay(BESIDE, BESIDE, 1, paired, everything, 2, core_sem).wait_send()


def one_row(query_in, key_in, value_in, block_keep):
    rows, width = query_in.shape
    heads = width // HD
    heads_a_chunk = HEADS_A_CHUNK
    chunks = heads // heads_a_chunk
    return pl.pallas_call(
        functools.partial(row_kernel, lax.axis_size("ctx"), heads_a_chunk),
        out_shape=pltpu.VMEM((rows, width), jnp.bfloat16),
        in_specs=[pl.BlockSpec(memory_space=pl.ANY)] * 4,
        out_specs=pl.BlockSpec(memory_space=pltpu.VMEM),
        scratch_shapes=[
            pltpu.VMEM((rows, width), jnp.bfloat16),
            pltpu.VMEM((2, 6 * rows, width), jnp.bfloat16),
            pltpu.SMEM((1, 3, 3) + block_keep.shape[1:3], jnp.int32),
            pltpu.SemaphoreType.DMA((4,)),
            pltpu.SemaphoreType.DMA((4,)),
            pltpu.SemaphoreType.DMA,
            pltpu.SemaphoreType.DMA((2, chunks)),
            pltpu.SemaphoreType.DMA((chunks,)),
            pltpu.SemaphoreType.DMA((chunks,)),
        ],
        compiler_params=pltpu.CompilerParams(
            collective_id=0, has_side_effects=True, vmem_limit_bytes=VMEM_LIMIT
        ),
        cost_estimate=pl.CostEstimate(
            flops=24 * rows * rows * width,
            bytes_accessed=10 * rows * width,
            transcendentals=6 * rows * rows * heads,
        ),
    )(query_in, key_in, value_in, block_keep.transpose(0, 3, 4, 1, 2))


def solution(mesh):
    in_one_row = mesh.shape["ctx"] == COLS // TILE_S
    return jax.shard_map(
        one_row if in_one_row else local,
        mesh=mesh,
        in_specs=(
            P(("clips", "ctx", "head"), None),
            P(("clips", "ctx", "head"), None),
            P(("clips", "ctx", "head"), None),
            P("clips", None, None, None, None),
        ),
        out_specs=P(("clips", "ctx", "head"), None),
        check_vma=False,
    )
```

```python
import functools

import jax
import jax.numpy as jnp
from jax import lax
from jax.experimental import pallas as pl
from jax.experimental.pallas import tpu as pltpu
from jax.sharding import PartitionSpec as P

HD = 128
TILE_S = 8
COLS = 64


NEG_BIG = -1e30


def swapped(block, axis, distance):
    count = lax.axis_size(axis)
    route = []
    for low in range(count):
        high = low | 1 << distance
        if high != low and high < count:
            route += [(low, high), (high, low)]
    return lax.ppermute(block, axis, route)


def from_behind(block, axis, distance):
    devices = range(lax.axis_size(axis))
    route = [(i - distance, i) for i in devices if i - distance in devices]
    return lax.ppermute(block, axis, route)


def order_pair(pair_side, mine, partner):
    first = jnp.where(pair_side == 0, mine, partner)
    second = jnp.where(pair_side == 0, partner, mine)
    return jnp.concatenate([first, second], axis=0)


def tile_flag(keep_pair, frame_at, col_at, frame_tiles, col_tiles, query_pos, frame_step, column):
    spot = column - query_pos + 1
    if frame_step == 1 and spot == 1:
        return jnp.array(True)
    frame_ok = (frame_at + frame_step - 1 >= 0) & (frame_at + frame_step - 1 < frame_tiles)
    col_ok = (col_at + column >= 0) & (col_at + column < col_tiles)
    return keep_pair[query_pos, frame_step, spot] & frame_ok & col_ok


def absorb(running, scores, allowed, mix_values):
    run_max, run_sum, run_out = running
    masked = jnp.where(allowed[None], scores, NEG_BIG)
    new_max = jnp.maximum(run_max, masked.max(-1))
    block_sum = jnp.where(allowed[None], jnp.exp(masked - new_max[..., None]), 0.0).sum(-1)
    weights_b = jnp.where(allowed[None], jnp.exp(masked - new_max[..., None]), 0.0).astype(
        jnp.bfloat16
    )
    factor = jnp.exp(run_max - new_max)
    new_sum = run_sum * factor + block_sum
    product = mix_values(weights_b)
    return (new_max, new_sum, run_out * factor[..., None] + product)


def inner_block(running, query_heads, key_pair, value_pair, tile_flags):
    tile_tok = key_pair.shape[0] // 2
    head_count = query_heads.shape[1]
    allowed = jnp.broadcast_to(tile_flags[:, None, :, None], (2, tile_tok, 2, tile_tok)).reshape(
        2 * tile_tok, 2 * tile_tok
    )
    key_rows = key_pair.reshape(2 * tile_tok, head_count, HD)
    value_rows = value_pair.reshape(2 * tile_tok, head_count, HD)
    scores = jnp.einsum(
        "qhd,khd->hqk", query_heads, key_rows, preferred_element_type=jnp.float32
    ) * HD ** (-0.5)

    def mix_values(weights_b):
        return jnp.einsum("hqk,khd->hqd", weights_b, value_rows, preferred_element_type=jnp.float32)

    return absorb(running, scores, allowed, mix_values)


def outer_block(running, query_heads, key_groups, value_groups, tile_flags):
    tile_tok = key_groups.shape[1]
    head_count = query_heads.shape[1]
    allowed = jnp.broadcast_to(tile_flags[:, None, None], (2, tile_tok, tile_tok)).reshape(
        2 * tile_tok, tile_tok
    )
    query_groups = query_heads.reshape(2, tile_tok, head_count, HD)
    key_rows = key_groups.reshape(2, tile_tok, head_count, HD)
    value_rows = value_groups.reshape(2, tile_tok, head_count, HD)
    scores = jnp.einsum(
        "gqhd,gkhd->hgqk", query_groups, key_rows, preferred_element_type=jnp.float32
    ) * HD ** (-0.5)
    scores = scores.reshape(head_count, 2 * tile_tok, tile_tok)

    def mix_values(weights_b):
        grouped = weights_b.reshape(head_count, 2, tile_tok, tile_tok)
        mixed = jnp.einsum(
            "hgqk,gkhd->hgqd", grouped, value_rows, preferred_element_type=jnp.float32
        )
        return mixed.reshape(head_count, 2 * tile_tok, HD)

    return absorb(running, scores, allowed, mix_values)


def local(query_in, key_in, value_in, block_keep):
    ctx_count = lax.axis_size("ctx")
    ctx_place = lax.axis_index("ctx")
    col_tiles = COLS // TILE_S
    row_tiles = max(1, ctx_count // (4 * col_tiles))
    frame_tiles = ctx_count // (row_tiles * col_tiles)
    frame_stride = row_tiles * col_tiles
    query_full, key_full, value_full = (
        lax.all_to_all(query_in, "head", split_axis=1, concat_axis=0, tiled=True),
        lax.all_to_all(key_in, "head", split_axis=1, concat_axis=0, tiled=True),
        lax.all_to_all(value_in, "head", split_axis=1, concat_axis=0, tiled=True),
    )
    tile_tok = query_full.shape[0]
    half_width = query_full.shape[1] // 2
    head_count = half_width // HD
    pair_side = ctx_place % 2

    def part_of(array, which):
        return lax.dynamic_slice_in_dim(array, which * half_width, half_width, 1)

    other_side = 1 - pair_side
    got_query, got_key, got_value = swapped(
        (
            part_of(query_full, other_side),
            part_of(key_full, other_side),
            part_of(value_full, other_side),
        ),
        "ctx",
        0,
    )
    query_pair = order_pair(pair_side, part_of(query_full, pair_side), got_query)
    key_pair = order_pair(pair_side, part_of(key_full, pair_side), got_key)
    value_pair = order_pair(pair_side, part_of(value_full, pair_side), got_value)
    query_heads = query_pair.reshape(2 * tile_tok, head_count, HD)
    first_tile = ctx_place - pair_side
    frame_at = first_tile // frame_stride
    col_at = first_tile % col_tiles
    keep_all = (block_keep > 0).reshape(-1, 3, 3)
    keep_pair = lax.dynamic_slice_in_dim(keep_all, first_tile, 2, 0)

    def inner_flags(frame_step):
        rows_list = []
        for query_pos in (0, 1):
            rows_list.append(
                jnp.stack(
                    [
                        tile_flag(
                            keep_pair,
                            frame_at,
                            col_at,
                            frame_tiles,
                            col_tiles,
                            query_pos,
                            frame_step,
                            column,
                        )
                        for column in (0, 1)
                    ]
                )
            )
        return jnp.stack(rows_list)

    def outer_flags(frame_step):
        left_flag = tile_flag(
            keep_pair, frame_at, col_at, frame_tiles, col_tiles, 0, frame_step, -1
        )
        right_flag = tile_flag(
            keep_pair, frame_at, col_at, frame_tiles, col_tiles, 1, frame_step, 2
        )
        return jnp.stack([left_flag, right_flag])

    side_tiles = []
    for distance, which_tile in ((2, 1), (-2, 0)):
        sent_tile = (
            key_pair[which_tile * tile_tok : (which_tile + 1) * tile_tok],
            value_pair[which_tile * tile_tok : (which_tile + 1) * tile_tok],
        )
        side_tiles.append(from_behind((sent_tile[0], sent_tile[1]), "ctx", distance))
    left_tile, right_tile = side_tiles
    running = (
        jnp.full((head_count, 2 * tile_tok), NEG_BIG, jnp.float32),
        jnp.zeros((head_count, 2 * tile_tok), jnp.float32),
        jnp.zeros((head_count, 2 * tile_tok, HD), jnp.float32),
    )
    running = inner_block(running, query_heads, key_pair, value_pair, inner_flags(1))
    running = outer_block(
        running,
        query_heads,
        jnp.stack([left_tile[0], right_tile[0]]),
        jnp.stack([left_tile[1], right_tile[1]]),
        outer_flags(1),
    )
    for frame_step, distance in ((0, frame_stride), (2, -frame_stride)):
        near_key, near_value = from_behind((key_pair, value_pair), "ctx", distance)
        corners = []
        for offset, which_tile in ((2, 1), (-2, 0)):
            sent_tile = (
                key_pair[which_tile * tile_tok : (which_tile + 1) * tile_tok],
                value_pair[which_tile * tile_tok : (which_tile + 1) * tile_tok],
            )
            corners.append(from_behind((sent_tile[0], sent_tile[1]), "ctx", distance + offset))
        running = inner_block(running, query_heads, near_key, near_value, inner_flags(frame_step))
        running = outer_block(
            running,
            query_heads,
            jnp.stack([corners[0][0], corners[1][0]]),
            jnp.stack([corners[0][1], corners[1][1]]),
            outer_flags(frame_step),
        )
    run_max, run_sum, run_out = running
    finished = (run_out / run_sum[..., None]).astype(jnp.bfloat16)
    finished = finished.transpose(1, 0, 2).reshape(2 * tile_tok, head_count * HD)
    first_out = finished[:tile_tok]
    second_out = finished[tile_tok:]
    mine_out = jnp.where(pair_side == 0, first_out, second_out)
    partner_out = jnp.where(pair_side == 0, second_out, first_out)
    returned = swapped(partner_out, "ctx", 0)
    whole_tile = jnp.where(
        pair_side == 0,
        jnp.concatenate([mine_out, returned], axis=1),
        jnp.concatenate([returned, mine_out], axis=1),
    )
    return lax.all_to_all(whole_tile, "head", split_axis=0, concat_axis=1, tiled=True)


HEADS_A_CHUNK = 1
FAR_LAG = 3
ATTEND_LAG = 5
VMEM_LIMIT = 60 * 2**20
LOG2_E = 1.4426950408889634
MESH = pl.DeviceIdType.MESH
OWN, CORE, BESIDE, FAR, BESIDE_CORE, FAR_CORE = range(6)


def attend(query, keys, values, beside_ok, far_ok, rows):
    scale = HD ** (-0.5) * LOG2_E
    scores = lax.dot_general(
        query, keys, (((1,), (1,)), ((), ())), preferred_element_type=jnp.float32
    )
    halves = [scores[:, slot * rows : (slot + 1) * rows] for slot in range(6)]
    own = jnp.maximum(halves[OWN], halves[CORE])
    beside = jnp.maximum(halves[BESIDE], halves[BESIDE_CORE])
    far = jnp.maximum(halves[FAR], halves[FAR_CORE])
    row_max = jnp.maximum(
        own, jnp.maximum(jnp.where(beside_ok, beside, NEG_BIG), jnp.where(far_ok, far, NEG_BIG))
    ).max(-1, keepdims=True)
    beside_max = jnp.where(beside_ok, row_max, -NEG_BIG)
    far_max = jnp.where(far_ok, row_max, -NEG_BIG)
    tops = (row_max, row_max, beside_max, far_max, beside_max, far_max)
    weights = [jnp.exp2((half - top) * scale) for half, top in zip(halves, tops)]
    row_sum = sum(weights[1:], weights[0]).sum(-1, keepdims=True)
    weights_b = jnp.concatenate([w.astype(jnp.bfloat16) for w in weights], axis=1)
    mixed = jnp.dot(weights_b, values, preferred_element_type=jnp.float32)
    return (mixed / row_sum).astype(jnp.bfloat16)


def row_kernel(
    tiles, heads_a_chunk,
    query_in, key_in, value_in, keep_in, result,
    query, pairs, keep, load_sem, send_sem, core_sem, paired_sem, far_sem, relay_sem,
):
    rows = query_in.shape[0]
    chunks = query_in.shape[1] // (heads_a_chunk * HD)
    width = heads_a_chunk * HD
    clip, tile, core = lax.axis_index("clips"), lax.axis_index("ctx"), lax.axis_index("head")
    side = lax.rem(tile, 2)
    step = 2 - 4 * side
    to_far, from_far = tile + step, tile - step
    sends_far = jnp.logical_and(to_far >= 0, to_far < tiles)
    gets_far = jnp.logical_and(from_far >= 0, from_far < tiles)
    other_core = (clip, tile, 1 - core)
    paired = (clip, tile + 1 - 2 * side, core)
    beyond = (clip, jnp.where(sends_far, to_far, tile + 1 - 2 * side), core)
    behind = (clip, jnp.where(gets_far, from_far, tile + 1 - 2 * side), core)

    def place(slot, count=1):
        return pl.ds(slot * rows, count * rows)

    def columns(chunk):
        return pl.ds(pl.multiple_of(chunk * width, width), width)

    everything = slice(None)

    def own_copy(which, slot, device, at, sender, receiver):
        return pltpu.make_async_remote_copy(
            src_ref=(key_in, value_in)[which].at[:, at],
            dst_ref=pairs.at[which, place(slot), at],
            send_sem=send_sem.at[sender],
            recv_sem=receiver,
            device_id=device,
            device_id_type=MESH,
        )

    def relay(source, slot, count, device, at, sender, receiver, which=everything):
        return pltpu.make_async_remote_copy(
            src_ref=pairs.at[which, place(source, count), at],
            dst_ref=pairs.at[which, place(slot, count), at],
            send_sem=send_sem.at[sender],
            recv_sem=receiver,
            device_id=device,
            device_id_type=MESH,
        )

    def to_far_tile(chunk, which=everything):
        return relay(BESIDE, FAR, 1, beyond, columns(chunk), 2, far_sem.at[chunk], which)

    def to_other_core(chunk, slot, count=1):
        return relay(
            slot, slot + 2, count, other_core, columns(chunk), 3, relay_sem.at[chunk]
        )

    def both_arrived(slot, at, receiver):
        relay(slot, slot, 1, paired, at, 0, receiver).wait_recv()

    loads = (
        pltpu.make_async_copy(keep_in, keep, load_sem.at[3]),
        pltpu.make_async_copy(query_in, query, load_sem.at[0]),
        pltpu.make_async_copy(key_in, pairs.at[0, place(OWN)], load_sem.at[1]),
        pltpu.make_async_copy(value_in, pairs.at[1, place(OWN)], load_sem.at[2]),
    )

    barrier = pltpu.get_barrier_semaphore()
    pl.semaphore_signal(barrier, inc=1, device_id=paired, device_id_type=MESH)

    @pl.when(sends_far)
    def _():
        pl.semaphore_signal(barrier, inc=1, device_id=beyond, device_id_type=MESH)

    @pl.when(gets_far)
    def _():
        pl.semaphore_signal(barrier, inc=1, device_id=behind, device_id_type=MESH)

    pl.semaphore_signal(barrier, inc=1, device_id=other_core, device_id_type=MESH)

    loads[0].start()

    @pl.when(jnp.logical_not(gets_far))
    def _():
        pairs[:, place(FAR), :] = jnp.zeros((2, rows, pairs.shape[2]), pairs.dtype)

    pl.semaphore_wait(
        barrier, 2 + sends_far.astype(jnp.int32) + gets_far.astype(jnp.int32)
    )

    for which in range(2):
        own_copy(which, CORE, other_core, everything, 1, core_sem).start()

    @pl.loop(0, chunks)
    def _(chunk):
        for which in range(2):
            own_copy(which, BESIDE, paired, columns(chunk), 0, paired_sem.at[which, chunk]).start()

    for load in loads[1:]:
        load.start()

    loads[0].wait()
    beside_ok = jnp.where(side == 0, keep[0, 1, 2, 0, tile], keep[0, 1, 0, 0, tile]) > 0
    far_ok = jnp.logical_and(
        jnp.where(side == 0, keep[0, 1, 0, 0, tile], keep[0, 1, 2, 0, tile]) > 0, gets_far
    )
    @pl.loop(0, chunks + ATTEND_LAG)
    def _(turn):
        @pl.when(turn < chunks)
        def _():
            for which in range(2):
                own_copy(
                    which, BESIDE, paired, columns(turn), 0, paired_sem.at[which, turn]
                ).wait_recv()

                @pl.when(sends_far)
                def _():
                    to_far_tile(turn, which).start()

            to_other_core(turn, BESIDE).start()

        @pl.when(jnp.logical_and(turn >= FAR_LAG, turn < chunks + FAR_LAG))
        def _():
            @pl.when(gets_far)
            def _():
                to_far_tile(turn - FAR_LAG).wait_recv()

            to_other_core(turn - FAR_LAG, FAR).start()

        @pl.when(turn == ATTEND_LAG)
        def _():
            for load in loads[1:]:
                load.wait()
            both_arrived(CORE, everything, core_sem)

        @pl.when(turn >= ATTEND_LAG)
        def _():
            chunk = turn - ATTEND_LAG
            to_other_core(chunk, BESIDE, 2).wait_recv()
            for head in range(heads_a_chunk):
                at = pl.ds(pl.multiple_of(chunk * width + head * HD, HD), HD)
                result[:, at] = attend(
                    query[:, at], pairs[0, :, at], pairs[1, :, at], beside_ok, far_ok, rows
                )

    relay(BESIDE, BESIDE, 1, paired, everything, 0, core_sem).wait_send()
    relay(BESIDE, BESIDE, 1, paired, everything, 1, core_sem).wait_send()
    relay(BESIDE, BESIDE, 2, paired, everything, 3, core_sem).wait_send()

    @pl.when(sends_far)
    def _():
        relay(BESIDE, BESIDE, 1, paired, everything, 2, core_sem).wait_send()


def one_row(query_in, key_in, value_in, block_keep):
    rows, width = query_in.shape
    heads = width // HD
    heads_a_chunk = HEADS_A_CHUNK
    chunks = heads // heads_a_chunk
    return pl.pallas_call(
        functools.partial(row_kernel, lax.axis_size("ctx"), heads_a_chunk),
        out_shape=pltpu.VMEM((rows, width), jnp.bfloat16),
        in_specs=[pl.BlockSpec(memory_space=pl.ANY)] * 4,
        out_specs=pl.BlockSpec(memory_space=pltpu.VMEM),
        scratch_shapes=[
            pltpu.VMEM((rows, width), jnp.bfloat16),
            pltpu.VMEM((2, 6 * rows, width), jnp.bfloat16),
            pltpu.SMEM((1, 3, 3) + block_keep.shape[1:3], jnp.int32),
            pltpu.SemaphoreType.DMA((4,)),
            pltpu.SemaphoreType.DMA((4,)),
            pltpu.SemaphoreType.DMA,
            pltpu.SemaphoreType.DMA((2, chunks)),
            pltpu.SemaphoreType.DMA((chunks,)),
            pltpu.SemaphoreType.DMA((chunks,)),
        ],
        compiler_params=pltpu.CompilerParams(
            collective_id=0, has_side_effects=True, vmem_limit_bytes=VMEM_LIMIT
        ),
        cost_estimate=pl.CostEstimate(
            flops=24 * rows * rows * width,
            bytes_accessed=10 * rows * width,
            transcendentals=6 * rows * rows * heads,
        ),
    )(query_in, key_in, value_in, block_keep.transpose(0, 3, 4, 1, 2))


def solution(mesh):
    in_one_row = mesh.shape["ctx"] == COLS // TILE_S
    return jax.shard_map(
        one_row if in_one_row else local,
        mesh=mesh,
        in_specs=(
            P(("clips", "ctx", "head"), None),
            P(("clips", "ctx", "head"), None),
            P(("clips", "ctx", "head"), None),
            P("clips", None, None, None, None),
        ),
        out_specs=P(("clips", "ctx", "head"), None),
        check_vma=False,
    )
```
